512 devices in a mesh: dp: 256 (over x, z, y), cent: 2 (over core).
Axes of the slice: x: 4, y: 8, z: 8, core: 2. Of those that a mesh axis runs over, the one named last changes fastest.
Arguments:
- tokens: float32 [30720, 128], P('dp'), may hold values from -6 to 6
- centroids: float32 [32768, 128], P(('dp', 'cent')), may hold values from -6 to 6
Outputs:
- new_centroids: float32 [32768, 128], P(('dp', 'cent'))
- residuals: float32 [30720, 128], P('dp')
The draws below stay inside these ranges and needn't reach their ends.
All inputs are finite; a program needn't handle non-finite values.
Results may differ from the reference program's by a relative error of at most 0.0005.
The reference program's roundings to bfloat16 on the way count: a program that leaves them out, or rounds other values in their place, can miss the bound.
Values may be sent and summed in bfloat16 or wider, within the bound.
A program may use at most 64 MiB of HBM per device.

```python
import jax
import jax.numpy as jnp
from jax import lax

EMBED_WIDTH = 128
K = 32768
ITERS = 3
KB = 2048
TOKENS = 30720


def levels(rng, dims, pieces, low, top_value):
    def one(dim, blocks):
        heights = jax.random.uniform(jax.random.fold_in(jax.random.fold_in(rng, 6), dim), (blocks,), jnp.float32, low / len(pieces), top_value / len(pieces))
        return jnp.repeat(jnp.exp(heights), dims[dim] // blocks).reshape((-1,) + (1,) * (len(dims) - dim - 1))

    loudness = one(*pieces[0])
    for cut in pieces[1:]:
        loudness = loudness * one(*cut)
    return loudness


def scatter_about(rng, shape, spread, limit, cuts=(), kind=jnp.bfloat16):
    loudness = levels(rng, shape, cuts, -0.22, 0.18) if cuts else 1.0
    entries = jax.random.normal(rng, shape, jnp.float32) * spread * loudness
    return jnp.minimum(jnp.maximum(entries, -limit), limit).astype(kind)


def setup_inputs(seed: int = 0) -> dict:
    streams_of = jax.random.split(jax.random.key(seed), 3)
    return {
        "tokens": scatter_about(streams_of[0], (TOKENS, EMBED_WIDTH), 1.0, 6.0, ((0, 256),), jnp.float32),
        "centroids": scatter_about(streams_of[1], (K, EMBED_WIDTH), 1.0, 6.0, ((0, 512),), jnp.float32),
    }


EPSILON = 1e-06
SOFTMAX_WARMTH = 0.05

def normalized_rows(values):
    return values * lax.rsqrt(lax.optimization_barrier(jnp.mean(values * values, axis=-1, keepdims=True)) + EPSILON)

def exponent_block(token_half_rows, block):
    affinity_scores = lax.dot_general(token_half_rows, block, (((1,), (1,)), ((), ())), preferred_element_type=jnp.float32)
    return jnp.exp((affinity_scores / EMBED_WIDTH - 1.0) / SOFTMAX_WARMTH)

def reference(tokens, centroids):
    unit_tok = normalized_rows(tokens)
    token_half_rows = unit_tok.astype(jnp.bfloat16)
    cen_bf = normalized_rows(centroids).astype(jnp.bfloat16)
    blocks = cen_bf.reshape(K // KB, KB, EMBED_WIDTH)
    col_mass = TOKENS / K
    scales = jnp.ones((K // KB, KB), jnp.float32)
    assignment_weight = jnp.ones((TOKENS,), jnp.float32)
    for step_index in range(ITERS):

        def row_step(total, packed):
            kernel = exponent_block(token_half_rows, packed[0])
            return (total + lax.optimization_barrier(jnp.sum(kernel * packed[1][None, :], axis=1)), None)
        row_sum = lax.scan(row_step, jnp.zeros((TOKENS,), jnp.float32), (blocks, scales))[0]
        assignment_weight = 1.0 / row_sum

        def col_only(block):
            kernel = exponent_block(token_half_rows, block)
            return lax.optimization_barrier(jnp.sum(kernel * assignment_weight[:, None], axis=0))
        col_sum = lax.map(col_only, blocks)
        scales = col_mass / col_sum
    weights_bf = assignment_weight.astype(jnp.bfloat16)

    def sum_block(block):
        kernel = exponent_block(token_half_rows, block)
        assign_bf = (kernel * weights_bf.astype(jnp.float32)[:, None]).astype(jnp.bfloat16)
        return lax.dot_general(assign_bf, token_half_rows, (((0,), (0,)), ((), ())), preferred_element_type=jnp.float32)
    sums = lax.map(sum_block, blocks)
    new_centroids = normalized_rows(sums.reshape(K, EMBED_WIDTH))
    new_blocks = new_centroids.astype(jnp.bfloat16).reshape(K // KB, KB, EMBED_WIDTH)

    def soft_step(total, packed):
        kernel = exponent_block(token_half_rows, packed[0])
        transport_plan_half = (kernel * assignment_weight[:, None] * packed[1][None, :]).astype(jnp.bfloat16)
        return (total + jnp.dot(transport_plan_half, packed[2], preferred_element_type=jnp.float32), None)
    soft = lax.scan(soft_step, jnp.zeros((TOKENS, EMBED_WIDTH), jnp.float32), (blocks, scales, new_blocks))[0]
    return (new_centroids, unit_tok - soft)
```

```python
import functools
import math

import jax
import jax.numpy as jnp
from jax import lax
from jax.experimental import pallas as pl
from jax.experimental.pallas import tpu as pltpu
from jax.sharding import PartitionSpec as P

ITERS = 3
EPSILON = 1e-06
SOFTMAX_WARMTH = 0.05
LANES = 128
HALF = 64
SOFT_CHUNKS = 4
MESH = pl.DeviceIdType.MESH


def layout(dp_size):
    if dp_size == 256:
        return 4, 8, 8, 2, 2
    return 2, 2, dp_size // 4, 1, 1


def normalized_rows(values):
    return values * lax.rsqrt(jnp.mean(values * values, axis=-1, keepdims=True) + EPSILON)


def lane_sums(values):
    total = values[:, :LANES]
    for g in range(1, values.shape[1] // LANES):
        total = total + values[:, g * LANES : (g + 1) * LANES]
    return jnp.sum(total.T, axis=0, keepdims=True)


def fused(
    dims,
    tok_ref,
    cen_ref,
    new_ref,
    res_ref,
    toks,
    toks_t,
    cens,
    kern,
    rows_mine,
    rows_pair,
    rows_in,
    weights,
    weight_cols,
    cols_in,
    cols_out,
    half_mat,
    sums_t,
    sums_out,
    sums_in,
    news,
    soft,
    soft_pair,
    soft_half,
    soft_in,
    soft_fin,
    send_sem,
    recv_sem,
):
    X, Y, Z, BY, BZ = dims
    NB = X * BY * BZ
    NA = (Y // BY) * (Z // BZ)
    rows_here = tok_ref.shape[0]
    width = NA * cen_ref.shape[0]
    groups = width // LANES
    col_mass = (rows_here * X * Y * Z) / (cen_ref.shape[0] * X * Y * Z * 2)

    dp = lax.axis_index("dp")
    core = lax.axis_index("cent")
    y = lax.rem(dp, Y)
    z = lax.rem(lax.div(dp, Y), Z)
    x = lax.div(dp, Y * Z)
    yb, ya = lax.rem(y, BY), lax.div(y, BY)
    zb, za = lax.rem(z, BZ), lax.div(z, BZ)
    AY, AZ = Y // BY, Z // BZ
    sibling = (dp, 1 - core)

    def row_peer(r):
        px = lax.rem(x + r // (BY * BZ), X)
        py = lax.rem(yb + (r // BZ) % BY, BY)
        pz = lax.rem(zb + r % BZ, BZ)
        return (px * Z + za * BZ + pz) * Y + ya * BY + py, (px * BY + py) * BZ + pz

    def col_peer(r):
        py = lax.rem(ya + r // AZ, AY)
        pz = lax.rem(za + r % AZ, AZ)
        return (x * Z + pz * BZ + zb) * Y + py * BY + yb, py * AZ + pz

    row_peers = [row_peer(r) for r in range(NB)]
    col_peers = [col_peer(r) for r in range(NA)]
    mine_b = row_peers[0][1]
    mine_a = col_peers[0][1]
    row_ids = [(p[0], core) for p in row_peers]
    col_ids = [(p[0], core) for p in col_peers]

    barrier = pltpu.get_barrier_semaphore()
    greeted = row_ids[1:] + col_ids[1:] + [sibling]
    for peer in greeted:
        pl.semaphore_signal(barrier, inc=1, device_id=peer, device_id_type=MESH)

    def send(src, dst, phase, peer):
        copy = pltpu.make_async_remote_copy(
            src_ref=src,
            dst_ref=dst,
            send_sem=send_sem.at[phase],
            recv_sem=recv_sem.at[phase],
            device_id=peer,
            device_id_type=MESH,
        )
        copy.start()
        return copy

    def arrived(view, phase):
        pltpu.make_async_copy(view, view, recv_sem.at[phase]).wait()

    sent = []

    def depart(view, phase):
        sent.append((view, phase))

    phases = iter(range(64))

    unit_tok = normalized_rows(tok_ref[...])
    pad = jnp.zeros((LANES - rows_here, LANES), jnp.float32)
    toks[mine_b] = jnp.concatenate([unit_tok, pad], axis=0).astype(jnp.bfloat16)
    cens[mine_a] = normalized_rows(cen_ref[...]).astype(jnp.bfloat16)
    pl.semaphore_wait(barrier, len(greeted))
    tok_phase, cen_phase = next(phases), next(phases)
    for r in range(1, NA):
        send(cens.at[mine_a], cens.at[mine_a], cen_phase, col_ids[r])
    for r in range(1, NB):
        send(toks.at[mine_b], toks.at[mine_b], tok_phase, row_ids[r])
    arrived(cens.at[pl.ds(0, NA - 1)], cen_phase)
    depart(cens.at[pl.ds(0, NA - 1)], cen_phase)
    arrived(toks.at[pl.ds(0, NB - 1)], tok_phase)
    depart(toks.at[pl.ds(0, NB - 1)], tok_phase)

    slope = math.log2(math.e) / (SOFTMAX_WARMTH * LANES)
    offset = math.log2(math.e) / SOFTMAX_WARMTH
    columns = cens[...].reshape(width, LANES)

    def kernel_rows(b, carry):
        affinity = lax.dot_general(
            toks[b], columns, (((1,), (1,)), ((), ())), preferred_element_type=jnp.float32
        )
        kernel = jnp.exp2(affinity * slope - offset)
        kern[b] = kernel
        rows_mine[0, pl.ds(b, 1), :] = lane_sums(kernel)
        return carry

    lax.fori_loop(0, NB, kernel_rows, 0)

    valid = lax.broadcasted_iota(jnp.int32, (NB, LANES), 1) < rows_here
    scales = None
    for it in range(ITERS):
        if it:
            scale_rows = scales

            def scaled_rows(b, carry):
                total = kern[b, :, :LANES] * scale_rows[0:1, :]
                for g in range(1, groups):
                    total = total + kern[b, :, g * LANES : (g + 1) * LANES] * scale_rows[g : g + 1, :]
                rows_mine[it, pl.ds(b, 1), :] = lane_sums(total)
                return carry

            lax.fori_loop(0, NB, scaled_rows, 0)

        phase = next(phases)
        send(rows_mine.at[it], rows_pair.at[it], phase, sibling)
        if it == 0:
            def turn(b, carry):
                toks_t[b] = toks[b].astype(jnp.float32).T.astype(jnp.bfloat16)
                return carry

            lax.fori_loop(0, NB, turn, 0)
        arrived(rows_pair.at[it], phase)
        depart(rows_pair.at[it], phase)
        rows_in[it, 0] = rows_mine[it] + rows_pair[it]
        phase = next(phases)
        for r in range(1, NB):
            send(rows_in.at[it, 0], rows_in.at[it, r], phase, row_ids[r])
        arrived(rows_in.at[it, pl.ds(1, NB - 1)], phase)
        depart(rows_in.at[it, pl.ds(1, NB - 1)], phase)
        row_sum = jnp.sum(rows_in[it], axis=0)
        weights[...] = jnp.where(valid, 1.0 / row_sum, 0.0)

        def weighted_columns(b, totals):
            spread = jnp.broadcast_to(weights[pl.ds(b, 1), :], (LANES, LANES)).T
            weight_cols[b] = spread
            return tuple(
                totals[g]
                + jnp.sum(
                    (kern[b, :, g * LANES : (g + 1) * LANES] * spread).reshape(LANES // 8, 8, LANES), axis=0
                )
                for g in range(groups)
            )

        totals = lax.fori_loop(
            0, NB, weighted_columns, tuple(jnp.zeros((8, LANES), jnp.float32) for _ in range(groups))
        )
        for g in range(groups):
            cols_in[it, 0, g : g + 1, :] = jnp.sum(totals[g], axis=0, keepdims=True)
        col_phase = next(phases)
        for r in range(1, NA):
            send(cols_in.at[it, 0], cols_in.at[it, r], col_phase, col_ids[r])

        if it == ITERS - 1:
            def assign_rows(b, carry):
                spread = weight_cols[b].astype(jnp.bfloat16).astype(jnp.float32)
                for g in range(groups):
                    half_mat[b, :, g * LANES : (g + 1) * LANES] = (
                        kern[b, :, g * LANES : (g + 1) * LANES] * spread
                    ).astype(jnp.bfloat16)
                return carry

            lax.fori_loop(0, NB, assign_rows, 0)
            sums_t[...] = jnp.zeros_like(sums_t)

            def sum_rows(b, carry):
                sums_t[...] += jnp.dot(toks_t[b], half_mat[b], preferred_element_type=jnp.float32)
                return carry

            lax.fori_loop(0, NB, sum_rows, 0)
            per = LANES // cen_ref.shape[0]
            for g in range(groups):
                turned = sums_t[:, g * LANES : (g + 1) * LANES].T
                for part in range(per):
                    sums_out[g * per + part] = turned[part * HALF : (part + 1) * HALF, :]
            sums_phase = next(phases)
            for r in range(1, NA):
                send(sums_out.at[col_peers[r][1]], sums_in.at[r], sums_phase, col_ids[r])
            sums_in[0] = sums_out[mine_a]

        arrived(cols_in.at[it, pl.ds(1, NA - 1)], col_phase)
        depart(cols_in.at[it, pl.ds(1, NA - 1)], col_phase)
        scales = col_mass / jnp.sum(cols_in[it], axis=0)

    arrived(sums_in.at[pl.ds(1, NA - 1)], sums_phase)
    depart(sums_in.at[pl.ds(1, NA - 1)], sums_phase)
    new_own = normalized_rows(jnp.sum(sums_in[...], axis=0))
    new_ref[...] = new_own
    news[mine_a] = new_own.astype(jnp.bfloat16)
    phase = next(phases)
    for r in range(1, NA):
        send(news.at[mine_a], news.at[mine_a], phase, col_ids[r])

    last_scales = scales

    def plan_rows(b, carry):
        spread = weight_cols[b]
        for g in range(groups):
            half_mat[b, :, g * LANES : (g + 1) * LANES] = (
                kern[b, :, g * LANES : (g + 1) * LANES] * spread * last_scales[g : g + 1, :]
            ).astype(jnp.bfloat16)
        return carry

    lax.fori_loop(0, NB, plan_rows, 0)
    arrived(news.at[pl.ds(0, NA - 1)], phase)
    depart(news.at[pl.ds(0, NA - 1)], phase)
    fresh = news[...].reshape(width, LANES)

    chunk = max(NB // SOFT_CHUNKS, 1)
    pair_phases = []
    for first in range(0, NB, chunk):
        for r in range(first, first + chunk):
            block = jnp.dot(half_mat[row_peers[r][1]], fresh, preferred_element_type=jnp.float32)
            soft[0, r] = block[:HALF]
            soft[1, r] = block[HALF:]
        phase = next(phases)
        pair_phases.append(phase)
        send(soft.at[1 - core, pl.ds(first, chunk)], soft_pair.at[pl.ds(first, chunk)], phase, sibling)
    soft_phase = next(phases)
    for first, phase in zip(range(0, NB, chunk), pair_phases):
        arrived(soft_pair.at[pl.ds(first, chunk)], phase)
        depart(soft_pair.at[pl.ds(first, chunk)], phase)
        for r in range(first, first + chunk):
            if r == 0:
                soft_in[0] = soft[core, 0] + soft_pair[0]
            else:
                soft_half[r] = soft[core, r] + soft_pair[r]
                send(soft_half.at[r], soft_in.at[r], soft_phase, row_ids[r])
    arrived(soft_in.at[pl.ds(1, NB - 1)], soft_phase)
    depart(soft_in.at[pl.ds(1, NB - 1)], soft_phase)
    soft_fin[core] = jnp.sum(soft_in[...], axis=0)
    phase = next(phases)
    send(soft_fin.at[core], soft_fin.at[core], phase, sibling)
    arrived(soft_fin.at[0], phase)
    depart(soft_fin.at[0], phase)
    whole = jnp.concatenate([soft_fin[0], soft_fin[1]], axis=0)
    res_ref[...] = normalized_rows(tok_ref[...]) - whole[:rows_here, :]
    for view, used in sent:
        pltpu.make_async_copy(view, view, send_sem.at[used]).wait()


def shards(dims, tokens, centroids):
    X, Y, Z, BY, BZ = dims
    NB = X * BY * BZ
    NA = (Y // BY) * (Z // BZ)
    width = NA * centroids.shape[0]
    groups = width // LANES
    f32, bf16 = jnp.float32, jnp.bfloat16
    scratch = [
        pltpu.VMEM((NB, LANES, LANES), bf16),
        pltpu.VMEM((NB, LANES, LANES), bf16),
        pltpu.VMEM((NA, HALF, LANES), bf16),
        pltpu.VMEM((NB, LANES, width), f32),
        pltpu.VMEM((ITERS, NB, LANES), f32),
        pltpu.VMEM((ITERS, NB, LANES), f32),
        pltpu.VMEM((ITERS, NB, NB, LANES), f32),
        pltpu.VMEM((NB, LANES), f32),
        pltpu.VMEM((NB, LANES, LANES), f32),
        pltpu.VMEM((ITERS, NA, groups, LANES), f32),
        pltpu.VMEM((8, LANES), f32),
        pltpu.VMEM((NB, LANES, width), bf16),
        pltpu.VMEM((LANES, width), f32),
        pltpu.VMEM((NA, HALF, LANES), f32),
        pltpu.VMEM((NA, HALF, LANES), f32),
        pltpu.VMEM((NA, HALF, LANES), bf16),
        pltpu.VMEM((2, NB, HALF, LANES), f32),
        pltpu.VMEM((NB, HALF, LANES), f32),
        pltpu.VMEM((NB, HALF, LANES), f32),
        pltpu.VMEM((NB, HALF, LANES), f32),
        pltpu.VMEM((2, HALF, LANES), f32),
        pltpu.SemaphoreType.DMA((24,)),
        pltpu.SemaphoreType.DMA((24,)),
    ]
    return pl.pallas_call(
        functools.partial(fused, dims),
        out_shape=(
            jax.ShapeDtypeStruct(centroids.shape, f32),
            jax.ShapeDtypeStruct(tokens.shape, f32),
        ),
        in_specs=[pl.BlockSpec(memory_space=pltpu.VMEM)] * 2,
        out_specs=[pl.BlockSpec(memory_space=pltpu.VMEM)] * 2,
        scratch_shapes=scratch,
        compiler_params=pltpu.CompilerParams(
            collective_id=0, has_side_effects=True, vmem_limit_bytes=48 * 1024 * 1024
        ),
        name="kmeans_step",
    )(tokens, centroids)


def solution(mesh):
    in_specs = (P("dp", None), P(("dp", "cent"), None))
    out_specs = (P(("dp", "cent"), None), P("dp", None))
    dims = layout(mesh.shape["dp"])
    return jax.shard_map(
        functools.partial(shards, dims), mesh=mesh, in_specs=in_specs, out_specs=out_specs, check_vma=False
    )
```

```python
import functools
import math

import jax
import jax.numpy as jnp
from jax import lax
from jax.experimental import pallas as pl
from jax.experimental.pallas import tpu as pltpu
from jax.sharding import PartitionSpec as P

ITERS = 3
EPSILON = 1e-06
SOFTMAX_WARMTH = 0.05
LANES = 128
HALF = 64
SOFT_CHUNKS = 4
MESH = pl.DeviceIdType.MESH


def layout(dp_size):
    if dp_size == 256:
        return 4, 8, 8, 2, 2
    return 2, 2, dp_size // 4, 1, 1


def nearest_first(size):
    return sorted(range(size), key=lambda step: min(step, size - step))


def normalized_rows(values):
    return values * lax.rsqrt(jnp.mean(values * values, axis=-1, keepdims=True) + EPSILON)


def lane_sums(values):
    total = values[:, :LANES]
    for g in range(1, values.shape[1] // LANES):
        total = total + values[:, g * LANES : (g + 1) * LANES]
    return jnp.sum(total.T, axis=0, keepdims=True)


def fused(
    dims,
    tok_ref,
    cen_ref,
    new_ref,
    res_ref,
    toks,
    toks_t,
    cens,
    kern,
    tile_acc,
    rows_mine,
    rows_pair,
    rows_in,
    weights,
    weight_cols,
    cols_in,
    half_mat,
    sums_out,
    sums_in,
    news,
    soft,
    soft_pair,
    soft_half,
    soft_in,
    soft_fin,
    send_sem,
    recv_sem,
):
    X, Y, Z, BY, BZ = dims
    AY, AZ = Y // BY, Z // BZ
    NB, NA = X * BY * BZ, AY * AZ
    rows_here = tok_ref.shape[0]
    panel = AZ * HALF
    groups = NA * HALF // LANES
    per_panel = panel // LANES
    many = min(NB, 4)
    col_mass = (rows_here * X * Y * Z) / (HALF * X * Y * Z * 2)

    dp = lax.axis_index("dp")
    core = lax.axis_index("cent")
    y = lax.rem(dp, Y)
    z = lax.rem(lax.div(dp, Y), Z)
    x = lax.div(dp, Y * Z)
    yb, ya = lax.rem(y, BY), lax.div(y, BY)
    zb, za = lax.rem(z, BZ), lax.div(z, BZ)
    sibling = (dp, 1 - core)

    def row_peer(r):
        px = lax.rem(x + r // (BY * BZ), X)
        py = lax.rem(yb + (r // BZ) % BY, BY)
        pz = lax.rem(zb + r % BZ, BZ)
        return (px * Z + za * BZ + pz) * Y + ya * BY + py, (px * BY + py) * BZ + pz

    def col_peer(r):
        py = lax.rem(ya + r // AZ, AY)
        pz = lax.rem(za + r % AZ, AZ)
        return (x * Z + pz * BZ + zb) * Y + py * BY + yb, py * AZ + pz

    row_peers = [row_peer(r) for r in range(NB)]
    col_peers = [col_peer(r) for r in range(NA)]
    mine_b = row_peers[0][1]
    mine_a = col_peers[0][1]
    row_ids = [(p[0], core) for p in row_peers]
    col_ids = [(p[0], core) for p in col_peers]
    steps = nearest_first(AY)
    panel_at = [lax.rem(ya + (AY - step) % AY, AY) for step in range(AY)]
    far_first = [step * AZ + other for step in reversed(steps) for other in reversed(nearest_first(AZ))]

    barrier = pltpu.get_barrier_semaphore()
    greeted = row_ids[1:] + col_ids[1:] + [sibling]
    for peer in greeted:
        pl.semaphore_signal(barrier, inc=1, device_id=peer, device_id_type=MESH)

    def send(src, dst, phase, peer):
        pltpu.make_async_remote_copy(
            src_ref=src,
            dst_ref=dst,
            send_sem=send_sem.at[phase],
            recv_sem=recv_sem.at[phase],
            device_id=peer,
            device_id_type=MESH,
        ).start()

    sent = []

    def arrived(view, phase):
        pltpu.make_async_copy(view, view, recv_sem.at[phase]).wait()
        sent.append((view, phase))

    phases = iter(range(32))

    def slot(b):
        return jnp.concatenate([toks[0, b], toks[1, b]], axis=0)

    pad = jnp.zeros((LANES - rows_here, LANES), jnp.float32)
    unit_tok = jnp.concatenate([normalized_rows(tok_ref[...]), pad], axis=0)
    toks[core, mine_b] = jnp.where(core == 0, unit_tok[:HALF], unit_tok[HALF:]).astype(jnp.bfloat16)
    cens[mine_a] = normalized_rows(cen_ref[...]).astype(jnp.bfloat16)
    pl.semaphore_wait(barrier, len(greeted))
    tok_phase, pair_phase = next(phases), next(phases)
    cen_phases = [next(phases) for _ in range(AY)]
    for r in range(1, NB):
        send(toks.at[core, mine_b], toks.at[core, mine_b], tok_phase, row_ids[r])
    for step in steps:
        for r in range(step * AZ, step * AZ + AZ):
            if r:
                send(cens.at[mine_a], cens.at[mine_a], cen_phases[step], col_ids[r])
    arrived(toks.at[0, pl.ds(0, NB - 1)], tok_phase)
    send(toks.at[core], toks.at[core], pair_phase, sibling)
    arrived(toks.at[0], pair_phase)

    slope = math.log2(math.e) / (SOFTMAX_WARMTH * LANES)
    offset = math.log2(math.e) / SOFTMAX_WARMTH
    for order, step in enumerate(steps):
        at = panel_at[step]
        arrived(cens.at[pl.ds(0, AZ - (step == 0))], cen_phases[step])
        columns = cens[pl.ds(at * AZ, AZ)].reshape(panel, LANES)

        def kernel_rows(i, carry):
            first = i * many
            block = jnp.concatenate([slot(first + j) for j in range(many)], axis=0)
            affinity = lax.dot_general(
                block, columns, (((1,), (1,)), ((), ())), preferred_element_type=jnp.float32
            )
            kernel = jnp.exp2(affinity * slope - offset)
            for j in range(many):
                part = kernel[j * LANES : (j + 1) * LANES]
                kern[at, first + j] = part
                total = part[:, :LANES]
                for h in range(1, per_panel):
                    total = total + part[:, h * LANES : (h + 1) * LANES]
                if order:
                    total = total + tile_acc[first + j]
                if order < AY - 1:
                    tile_acc[first + j] = total
                else:
                    rows_mine[0, pl.ds(first + j, 1), :] = jnp.sum(total.T, axis=0, keepdims=True)
            return carry

        lax.fori_loop(0, NB // many, kernel_rows, 0)

    def part_of(b, g):
        h = g % per_panel
        return kern[g // per_panel, b, :, h * LANES : (h + 1) * LANES]

    valid = lax.broadcasted_iota(jnp.int32, (NB, LANES), 1) < rows_here
    scales = None
    for it in range(ITERS):
        if it:
            scale_rows = scales

            def scaled_rows(b, carry):
                total = part_of(b, 0) * scale_rows[0:1, :]
                for g in range(1, groups):
                    total = total + part_of(b, g) * scale_rows[g : g + 1, :]
                rows_mine[it, pl.ds(b, 1), :] = jnp.sum(total.T, axis=0, keepdims=True)
                return carry

            lax.fori_loop(0, NB, scaled_rows, 0, unroll=many)

        phase = next(phases)
        send(rows_mine.at[it], rows_pair.at[it], phase, sibling)
        arrived(rows_pair.at[it], phase)
        rows_in[it, 0] = rows_mine[it] + rows_pair[it]
        phase = next(phases)
        for r in range(1, NB):
            send(rows_in.at[it, 0], rows_in.at[it, r], phase, row_ids[r])
        if it == 0:
            def turn(b, carry):
                place = pl.ds(pl.multiple_of(b * LANES, LANES), LANES)
                toks_t[:, place] = slot(b).astype(jnp.float32).T.astype(jnp.bfloat16)
                return carry

            lax.fori_loop(0, NB, turn, 0, unroll=many)
        arrived(rows_in.at[it, pl.ds(1, NB - 1)], phase)
        row_sum = jnp.sum(rows_in[it], axis=0)
        weights[...] = jnp.where(valid, 1.0 / row_sum, 0.0)

        def weighted_columns(b, totals):
            spread = jnp.broadcast_to(weights[pl.ds(b, 1), :], (LANES, LANES)).T
            weight_cols[b] = spread
            return tuple(
                totals[g] + jnp.sum((part_of(b, g) * spread).reshape(LANES // 8, 8, LANES), axis=0)
                for g in range(groups)
            )

        zeros = tuple(jnp.zeros((8, LANES), jnp.float32) for _ in range(groups))
        totals = lax.fori_loop(0, NB, weighted_columns, zeros, unroll=many)
        for g in range(groups):
            cols_in[it, 0, g : g + 1, :] = jnp.sum(totals[g], axis=0, keepdims=True)
        col_phase = next(phases)
        for r in far_first:
            if r:
                send(cols_in.at[it, 0], cols_in.at[it, r], col_phase, col_ids[r])

        if it == ITERS - 1:
            sums_phase = next(phases)
            for step in reversed(steps):
                at = lax.rem(ya + step, AY)

                def assign_rows(b, carry):
                    spread = weight_cols[b].astype(jnp.bfloat16).astype(jnp.float32)
                    for h in range(per_panel):
                        lanes = slice(h * LANES, (h + 1) * LANES)
                        half_mat[step, b, :, lanes] = (kern[at, b, :, lanes] * spread).astype(jnp.bfloat16)
                    return carry

                lax.fori_loop(0, NB, assign_rows, 0, unroll=many)
                turned = jnp.dot(
                    toks_t[...],
                    half_mat[step].reshape(NB * LANES, panel),
                    preferred_element_type=jnp.float32,
                )
                for h in range(per_panel):
                    pair = turned[:, h * LANES : (h + 1) * LANES].T
                    sums_out[at * AZ + 2 * h] = pair[:HALF]
                    sums_out[at * AZ + 2 * h + 1] = pair[HALF:]
                for r in far_first:
                    if r and r // AZ == step:
                        send(sums_out.at[col_peers[r][1]], sums_in.at[r], sums_phase, col_ids[r])
            sums_in[0] = sums_out[mine_a]

        arrived(cols_in.at[it, pl.ds(1, NA - 1)], col_phase)
        scales = col_mass / jnp.sum(cols_in[it], axis=0)

    last_scales = scales

    def plan_rows(b, carry):
        spread = weight_cols[b]
        for g in range(groups):
            h = g % per_panel
            half_mat[g // per_panel, b, :, h * LANES : (h + 1) * LANES] = (
                part_of(b, g) * spread * last_scales[g : g + 1, :]
            ).astype(jnp.bfloat16)
        return carry

    lax.fori_loop(0, NB, plan_rows, 0, unroll=many)

    arrived(sums_in.at[pl.ds(1, NA - 1)], sums_phase)
    new_own = normalized_rows(jnp.sum(sums_in[...], axis=0))
    news[mine_a] = new_own.astype(jnp.bfloat16)
    new_phases = [next(phases) for _ in range(AY)]
    for r in far_first:
        if r:
            send(news.at[mine_a], news.at[mine_a], new_phases[r // AZ], col_ids[r])
    new_ref[...] = new_own

    chunk = max(NB // SOFT_CHUNKS, 1)
    soft_phases = []
    for order, step in enumerate(steps):
        at = panel_at[step]
        arrived(news.at[pl.ds(0, AZ - (step == 0))], new_phases[step])
        fresh = news[pl.ds(at * AZ, AZ)].reshape(panel, LANES)
        if order < AY - 1:

            def soft_rows(i, carry):
                place = pl.ds(i * many, many)
                block = jnp.dot(
                    half_mat[at, place].reshape(many * LANES, panel), fresh, preferred_element_type=jnp.float32
                ).reshape(many, LANES, LANES)
                tile_acc[place] = block if order == 0 else tile_acc[place] + block
                return carry

            lax.fori_loop(0, NB // many, soft_rows, 0)
            continue
        for first in range(0, NB, chunk):
            block = jnp.dot(
                jnp.concatenate([half_mat[at, row_peers[r][1]] for r in range(first, first + chunk)], axis=0),
                fresh,
                preferred_element_type=jnp.float32,
            )
            for r in range(first, first + chunk):
                whole = block[(r - first) * LANES : (r - first + 1) * LANES] + tile_acc[row_peers[r][1]]
                soft[0, r] = whole[:HALF]
                soft[1, r] = whole[HALF:]
            phase = next(phases)
            soft_phases.append(phase)
            send(soft.at[1 - core, pl.ds(first, chunk)], soft_pair.at[pl.ds(first, chunk)], phase, sibling)
    soft_phase = next(phases)
    for first, phase in zip(range(0, NB, chunk), soft_phases):
        arrived(soft_pair.at[pl.ds(first, chunk)], phase)
        for r in range(first, first + chunk):
            if r == 0:
                soft_in[0] = soft[core, 0] + soft_pair[0]
            else:
                soft_half[r] = soft[core, r] + soft_pair[r]
                send(soft_half.at[r], soft_in.at[r], soft_phase, row_ids[r])
    arrived(soft_in.at[pl.ds(1, NB - 1)], soft_phase)
    soft_fin[core] = jnp.sum(soft_in[...], axis=0)
    phase = next(phases)
    send(soft_fin.at[core], soft_fin.at[core], phase, sibling)
    unit_tok = normalized_rows(tok_ref[...])
    arrived(soft_fin.at[0], phase)
    whole = jnp.concatenate([soft_fin[0], soft_fin[1]], axis=0)
    res_ref[...] = unit_tok - whole[:rows_here, :]
    for view, used in sent:
        pltpu.make_async_copy(view, view, send_sem.at[used]).wait()


def shards(dims, tokens, centroids):
    X, Y, Z, BY, BZ = dims
    AY, AZ = Y // BY, Z // BZ
    NB, NA = X * BY * BZ, AY * AZ
    panel = AZ * HALF
    groups = NA * HALF // LANES
    f32, bf16 = jnp.float32, jnp.bfloat16
    scratch = [
        pltpu.VMEM((2, NB, HALF, LANES), bf16),
        pltpu.VMEM((LANES, NB * LANES), bf16),
        pltpu.VMEM((NA, HALF, LANES), bf16),
        pltpu.VMEM((AY, NB, LANES, panel), f32),
        pltpu.VMEM((NB, LANES, LANES), f32),
        pltpu.VMEM((ITERS, NB, LANES), f32),
        pltpu.VMEM((ITERS, NB, LANES), f32),
        pltpu.VMEM((ITERS, NB, NB, LANES), f32),
        pltpu.VMEM((NB, LANES), f32),
        pltpu.VMEM((NB, LANES, LANES), f32),
        pltpu.VMEM((ITERS, NA, groups, LANES), f32),
        pltpu.VMEM((AY, NB, LANES, panel), bf16),
        pltpu.VMEM((NA, HALF, LANES), f32),
        pltpu.VMEM((NA, HALF, LANES), f32),
        pltpu.VMEM((NA, HALF, LANES), bf16),
        pltpu.VMEM((2, NB, HALF, LANES), f32),
        pltpu.VMEM((NB, HALF, LANES), f32),
        pltpu.VMEM((NB, HALF, LANES), f32),
        pltpu.VMEM((NB, HALF, LANES), f32),
        pltpu.VMEM((2, HALF, LANES), f32),
        pltpu.SemaphoreType.DMA((32,)),
        pltpu.SemaphoreType.DMA((32,)),
    ]
    return pl.pallas_call(
        functools.partial(fused, dims),
        out_shape=(
            jax.ShapeDtypeStruct(centroids.shape, f32),
            jax.ShapeDtypeStruct(tokens.shape, f32),
        ),
        in_specs=[pl.BlockSpec(memory_space=pltpu.VMEM)] * 2,
        out_specs=[pl.BlockSpec(memory_space=pltpu.VMEM)] * 2,
        scratch_shapes=scratch,
        compiler_params=pltpu.CompilerParams(
            collective_id=0, has_side_effects=True, vmem_limit_bytes=48 * 1024 * 1024
        ),
        name="kmeans_step",
    )(tokens, centroids)


def solution(mesh):
    in_specs = (P("dp", None), P(("dp", "cent"), None))
    out_specs = (P(("dp", "cent"), None), P("dp", None))
    dims = layout(mesh.shape["dp"])
    return jax.shard_map(
        functools.partial(shards, dims), mesh=mesh, in_specs=in_specs, out_specs=out_specs, check_vma=False
    )
```

```python
import functools
import math

import jax
import jax.numpy as jnp
from jax import lax
from jax.experimental import pallas as pl
from jax.experimental.pallas import tpu as pltpu
from jax.sharding import PartitionSpec as P

ITERS = 3
EPSILON = 1e-06
SOFTMAX_WARMTH = 0.05
LANES = 128
HALF = 64
SOFT_CHUNKS = 4
MESH = pl.DeviceIdType.MESH


def layout(dp_size):
    if dp_size == 256:
        return 4, 8, 8, 2, 2
    return 2, 2, dp_size // 4, 1, 1


def nearest_first(size):
    return sorted(range(size), key=lambda step: min(step, size - step))


def normalized_rows(values):
    return values * lax.rsqrt(jnp.mean(values * values, axis=-1, keepdims=True) + EPSILON)


def lane_sums(values):
    total = values[:, :LANES]
    for g in range(1, values.shape[1] // LANES):
        total = total + values[:, g * LANES : (g + 1) * LANES]
    return jnp.sum(total.T, axis=0, keepdims=True)


def fused(
    dims,
    tok_hbm,
    cen_hbm,
    new_ref,
    res_ref,
    tok_ref,
    cen_ref,
    toks,
    toks_t,
    cens,
    kern,
    tile_acc,
    rows_mine,
    rows_pair,
    rows_in,
    weights,
    weight_cols,
    cols_in,
    half_mat,
    sums_out,
    sums_in,
    news,
    soft,
    soft_pair,
    soft_half,
    soft_in,
    soft_fin,
    send_sem,
    recv_sem,
    load_sem,
):
    X, Y, Z, BY, BZ = dims
    AY, AZ = Y // BY, Z // BZ
    NB, NA = X * BY * BZ, AY * AZ
    rows_here = tok_ref.shape[0]
    load_tok = pltpu.make_async_copy(tok_hbm, tok_ref, load_sem.at[0])
    load_cen = pltpu.make_async_copy(cen_hbm, cen_ref, load_sem.at[1])
    load_tok.start()
    load_cen.start()
    panel = AZ * HALF
    groups = NA * HALF // LANES
    per_panel = panel // LANES
    many = min(NB, 4)
    col_mass = (rows_here * X * Y * Z) / (HALF * X * Y * Z * 2)

    dp = lax.axis_index("dp")
    core = lax.axis_index("cent")
    y = lax.rem(dp, Y)
    z = lax.rem(lax.div(dp, Y), Z)
    x = lax.div(dp, Y * Z)
    yb, ya = lax.rem(y, BY), lax.div(y, BY)
    zb, za = lax.rem(z, BZ), lax.div(z, BZ)
    sibling = (dp, 1 - core)

    def row_peer(r):
        px = lax.rem(x + r // (BY * BZ), X)
        py = lax.rem(yb + (r // BZ) % BY, BY)
        pz = lax.rem(zb + r % BZ, BZ)
        return (px * Z + za * BZ + pz) * Y + ya * BY + py, (px * BY + py) * BZ + pz

    def col_peer(r):
        py = lax.rem(ya + r // AZ, AY)
        pz = lax.rem(za + r % AZ, AZ)
        return (x * Z + pz * BZ + zb) * Y + py * BY + yb, py * AZ + pz

    row_peers = [row_peer(r) for r in range(NB)]
    col_peers = [col_peer(r) for r in range(NA)]
    mine_b = row_peers[0][1]
    mine_a = col_peers[0][1]
    row_ids = [(p[0], core) for p in row_peers]
    col_ids = [(p[0], core) for p in col_peers]
    steps = nearest_first(AY)
    panel_at = [lax.rem(ya + (AY - step) % AY, AY) for step in range(AY)]
    far_first = [step * AZ + other for step in reversed(steps) for other in reversed(nearest_first(AZ))]

    barrier = pltpu.get_barrier_semaphore()
    along_z = [r for r in nearest_first(AZ) if r]
    along_y = [step * AZ for step in steps if step]
    greeted = row_ids[1:] + [col_ids[r] for r in along_z + along_y] + [sibling]
    for peer in greeted:
        pl.semaphore_signal(barrier, inc=1, device_id=peer, device_id_type=MESH)

    def send(src, dst, phase, peer):
        pltpu.make_async_remote_copy(
            src_ref=src,
            dst_ref=dst,
            send_sem=send_sem.at[phase],
            recv_sem=recv_sem.at[phase],
            device_id=peer,
            device_id_type=MESH,
        ).start()

    sent = []

    def arrived(view, phase):
        pltpu.make_async_copy(view, view, recv_sem.at[phase]).wait()
        sent.append((view, phase))

    phases = iter(range(48))

    def slot(b):
        return jnp.concatenate([toks[0, b], toks[1, b]], axis=0)

    load_tok.wait()
    load_cen.wait()
    pad = jnp.zeros((LANES - rows_here, LANES), jnp.float32)
    unit_tok = jnp.concatenate([normalized_rows(tok_ref[...]), pad], axis=0)
    toks[core, mine_b] = jnp.where(core == 0, unit_tok[:HALF], unit_tok[HALF:]).astype(jnp.bfloat16)
    cens[mine_a] = normalized_rows(cen_ref[...]).astype(jnp.bfloat16)
    pl.semaphore_wait(barrier, len(greeted))
    tok_phase, pair_phase = next(phases), next(phases)
    z_phases = [next(phases) for _ in range(AZ)]
    cen_phases = [next(phases) for _ in range(AY)]
    for r in reversed(along_z):
        send(cens.at[mine_a], cens.at[mine_a], z_phases[r], col_ids[r])
    for r in reversed(along_y):
        send(cens.at[mine_a], cens.at[mine_a], cen_phases[r // AZ], col_ids[r])
    for r in range(1, NB):
        send(toks.at[core, mine_b], toks.at[core, mine_b], tok_phase, row_ids[r])
    for step in along_z:
        piece = ya * AZ + lax.rem(za + AZ - step, AZ)
        arrived(cens.at[0], z_phases[step])
        for r in reversed(along_y):
            send(cens.at[piece], cens.at[piece], cen_phases[r // AZ], col_ids[r])
    arrived(toks.at[0, pl.ds(0, NB - 1)], tok_phase)
    send(toks.at[core], toks.at[core], pair_phase, sibling)
    arrived(toks.at[0], pair_phase)

    slope = math.log2(math.e) / (SOFTMAX_WARMTH * LANES)
    offset = math.log2(math.e) / SOFTMAX_WARMTH
    for order, step in enumerate(steps):
        at = panel_at[step]
        if step:
            arrived(cens.at[pl.ds(0, AZ)], cen_phases[step])
        columns = cens[pl.ds(at * AZ, AZ)].reshape(panel, LANES)

        def kernel_rows(i, carry):
            first = i * many
            block = jnp.concatenate([slot(first + j) for j in range(many)], axis=0)
            affinity = lax.dot_general(
                block, columns, (((1,), (1,)), ((), ())), preferred_element_type=jnp.float32
            )
            kernel = jnp.exp2(affinity * slope - offset)
            for j in range(many):
                part = kernel[j * LANES : (j + 1) * LANES]
                kern[at, first + j] = part
                total = part[:, :LANES]
                for h in range(1, per_panel):
                    total = total + part[:, h * LANES : (h + 1) * LANES]
                if order:
                    total = total + tile_acc[first + j]
                if order < AY - 1:
                    tile_acc[first + j] = total
                else:
                    rows_mine[0, pl.ds(first + j, 1), :] = jnp.sum(total.T, axis=0, keepdims=True)
            return carry

        lax.fori_loop(0, NB // many, kernel_rows, 0)

    def part_of(b, g):
        h = g % per_panel
        return kern[g // per_panel, b, :, h * LANES : (h + 1) * LANES]

    valid = lax.broadcasted_iota(jnp.int32, (NB, LANES), 1) < rows_here
    scales = None
    for it in range(ITERS):
        if it:
            scale_rows = scales

            def scaled_rows(b, carry):
                total = part_of(b, 0) * scale_rows[0:1, :]
                for g in range(1, groups):
                    total = total + part_of(b, g) * scale_rows[g : g + 1, :]
                rows_mine[it, pl.ds(b, 1), :] = jnp.sum(total.T, axis=0, keepdims=True)
                return carry

            lax.fori_loop(0, NB, scaled_rows, 0, unroll=many)

        phase = next(phases)
        send(rows_mine.at[it], rows_pair.at[it], phase, sibling)
        arrived(rows_pair.at[it], phase)
        rows_in[it, 0] = rows_mine[it] + rows_pair[it]
        phase = next(phases)
        for r in range(1, NB):
            send(rows_in.at[it, 0], rows_in.at[it, r], phase, row_ids[r])
        if it == 0:
            def turn(b, carry):
                place = pl.ds(pl.multiple_of(b * LANES, LANES), LANES)
                toks_t[:, place] = slot(b).astype(jnp.float32).T.astype(jnp.bfloat16)
                return carry

            lax.fori_loop(0, NB, turn, 0, unroll=many)
        arrived(rows_in.at[it, pl.ds(1, NB - 1)], phase)
        row_sum = jnp.sum(rows_in[it], axis=0)
        weights[...] = jnp.where(valid, 1.0 / row_sum, 0.0)

        def weighted_columns(b, totals):
            spread = jnp.broadcast_to(weights[pl.ds(b, 1), :], (LANES, LANES)).T
            weight_cols[b] = spread
            return tuple(
                totals[g] + jnp.sum((part_of(b, g) * spread).reshape(LANES // 8, 8, LANES), axis=0)
                for g in range(groups)
            )

        zeros = tuple(jnp.zeros((8, LANES), jnp.float32) for _ in range(groups))
        totals = lax.fori_loop(0, NB, weighted_columns, zeros, unroll=many)
        for g in range(groups):
            cols_in[it, 0, g : g + 1, :] = jnp.sum(totals[g], axis=0, keepdims=True)
        col_phase = next(phases)
        for r in far_first:
            if r:
                send(cols_in.at[it, 0], cols_in.at[it, r], col_phase, col_ids[r])

        if it == ITERS - 1:
            sums_phase = next(phases)
            for step in reversed(steps):
                at = lax.rem(ya + step, AY)

                def assign_rows(b, carry):
                    spread = weight_cols[b].astype(jnp.bfloat16).astype(jnp.float32)
                    for h in range(per_panel):
                        lanes = slice(h * LANES, (h + 1) * LANES)
                        half_mat[step, b, :, lanes] = (kern[at, b, :, lanes] * spread).astype(jnp.bfloat16)
                    return carry

                lax.fori_loop(0, NB, assign_rows, 0, unroll=many)
                turned = jnp.dot(
                    toks_t[...],
                    half_mat[step].reshape(NB * LANES, panel),
                    preferred_element_type=jnp.float32,
                )
                for h in range(per_panel):
                    pair = turned[:, h * LANES : (h + 1) * LANES].T
                    sums_out[at * AZ + 2 * h] = pair[:HALF]
                    sums_out[at * AZ + 2 * h + 1] = pair[HALF:]
                for r in far_first:
                    if r and r // AZ == step:
                        send(sums_out.at[col_peers[r][1]], sums_in.at[r], sums_phase, col_ids[r])
            sums_in[0] = sums_out[mine_a]

        arrived(cols_in.at[it, pl.ds(1, NA - 1)], col_phase)
        scales = col_mass / jnp.sum(cols_in[it], axis=0)

    last_scales = scales

    def plan_rows(b, carry):
        spread = weight_cols[b]
        for g in range(groups):
            h = g % per_panel
            half_mat[g // per_panel, b, :, h * LANES : (h + 1) * LANES] = (
                part_of(b, g) * spread * last_scales[g : g + 1, :]
            ).astype(jnp.bfloat16)
        return carry

    lax.fori_loop(0, NB, plan_rows, 0, unroll=many)

    arrived(sums_in.at[pl.ds(1, NA - 1)], sums_phase)
    new_own = normalized_rows(jnp.sum(sums_in[...], axis=0))
    news[mine_a] = new_own.astype(jnp.bfloat16)
    new_phases = [next(phases) for _ in range(AY)]
    for r in far_first:
        if r:
            send(news.at[mine_a], news.at[mine_a], new_phases[r // AZ], col_ids[r])
    new_ref[...] = new_own

    chunk = max(NB // SOFT_CHUNKS, 1)
    soft_phases = []
    for order, step in enumerate(steps):
        at = panel_at[step]
        arrived(news.at[pl.ds(0, AZ - (step == 0))], new_phases[step])
        fresh = news[pl.ds(at * AZ, AZ)].reshape(panel, LANES)
        if order < AY - 1:

            def soft_rows(i, carry):
                place = pl.ds(i * many, many)
                block = jnp.dot(
                    half_mat[at, place].reshape(many * LANES, panel), fresh, preferred_element_type=jnp.float32
                ).reshape(many, LANES, LANES)
                tile_acc[place] = block if order == 0 else tile_acc[place] + block
                return carry

            lax.fori_loop(0, NB // many, soft_rows, 0)
            continue
        for first in range(0, NB, chunk):
            block = jnp.dot(
                jnp.concatenate([half_mat[at, row_peers[r][1]] for r in range(first, first + chunk)], axis=0),
                fresh,
                preferred_element_type=jnp.float32,
            )
            for r in range(first, first + chunk):
                whole = block[(r - first) * LANES : (r - first + 1) * LANES] + tile_acc[row_peers[r][1]]
                soft[0, r] = whole[:HALF]
                soft[1, r] = whole[HALF:]
            phase = next(phases)
            soft_phases.append(phase)
            send(soft.at[1 - core, pl.ds(first, chunk)], soft_pair.at[pl.ds(first, chunk)], phase, sibling)
    soft_phase = next(phases)
    for first, phase in zip(range(0, NB, chunk), soft_phases):
        arrived(soft_pair.at[pl.ds(first, chunk)], phase)
        for r in range(first, first + chunk):
            if r == 0:
                soft_in[0] = soft[core, 0] + soft_pair[0]
            else:
                soft_half[r] = soft[core, r] + soft_pair[r]
                send(soft_half.at[r], soft_in.at[r], soft_phase, row_ids[r])
    arrived(soft_in.at[pl.ds(1, NB - 1)], soft_phase)
    soft_fin[core] = jnp.sum(soft_in[...], axis=0)
    phase = next(phases)
    send(soft_fin.at[core], soft_fin.at[core], phase, sibling)
    unit_tok = normalized_rows(tok_ref[...])
    arrived(soft_fin.at[0], phase)
    whole = jnp.concatenate([soft_fin[0], soft_fin[1]], axis=0)
    res_ref[...] = unit_tok - whole[:rows_here, :]
    for view, used in sent:
        pltpu.make_async_copy(view, view, send_sem.at[used]).wait()


def shards(dims, tokens, centroids):
    X, Y, Z, BY, BZ = dims
    AY, AZ = Y // BY, Z // BZ
    NB, NA = X * BY * BZ, AY * AZ
    panel = AZ * HALF
    groups = NA * HALF // LANES
    f32, bf16 = jnp.float32, jnp.bfloat16
    scratch = [
        pltpu.VMEM(tokens.shape, f32),
        pltpu.VMEM(centroids.shape, f32),
        pltpu.VMEM((2, NB, HALF, LANES), bf16),
        pltpu.VMEM((LANES, NB * LANES), bf16),
        pltpu.VMEM((NA, HALF, LANES), bf16),
        pltpu.VMEM((AY, NB, LANES, panel), f32),
        pltpu.VMEM((NB, LANES, LANES), f32),
        pltpu.VMEM((ITERS, NB, LANES), f32),
        pltpu.VMEM((ITERS, NB, LANES), f32),
        pltpu.VMEM((ITERS, NB, NB, LANES), f32),
        pltpu.VMEM((NB, LANES), f32),
        pltpu.VMEM((NB, LANES, LANES), f32),
        pltpu.VMEM((ITERS, NA, groups, LANES), f32),
        pltpu.VMEM((AY, NB, LANES, panel), bf16),
        pltpu.VMEM((NA, HALF, LANES), f32),
        pltpu.VMEM((NA, HALF, LANES), f32),
        pltpu.VMEM((NA, HALF, LANES), bf16),
        pltpu.VMEM((2, NB, HALF, LANES), f32),
        pltpu.VMEM((NB, HALF, LANES), f32),
        pltpu.VMEM((NB, HALF, LANES), f32),
        pltpu.VMEM((NB, HALF, LANES), f32),
        pltpu.VMEM((2, HALF, LANES), f32),
        pltpu.SemaphoreType.DMA((48,)),
        pltpu.SemaphoreType.DMA((48,)),
        pltpu.SemaphoreType.DMA((2,)),
    ]
    return pl.pallas_call(
        functools.partial(fused, dims),
        out_shape=(
            jax.ShapeDtypeStruct(centroids.shape, f32),
            jax.ShapeDtypeStruct(tokens.shape, f32),
        ),
        in_specs=[pl.BlockSpec(memory_space=pl.ANY)] * 2,
        out_specs=[pl.BlockSpec(memory_space=pltpu.VMEM)] * 2,
        scratch_shapes=scratch,
        compiler_params=pltpu.CompilerParams(
            collective_id=0, has_side_effects=True, vmem_limit_bytes=48 * 1024 * 1024
        ),
        name="kmeans_step",
    )(tokens, centroids)


def solution(mesh):
    in_specs = (P("dp", None), P(("dp", "cent"), None))
    out_specs = (P(("dp", "cent"), None), P("dp", None))
    dims = layout(mesh.shape["dp"])
    return jax.shard_map(
        functools.partial(shards, dims), mesh=mesh, in_specs=in_specs, out_specs=out_specs, check_vma=False
    )
```

```python
import functools
import math

import jax
import jax.numpy as jnp
from jax import lax
from jax.experimental import pallas as pl
from jax.experimental.pallas import tpu as pltpu
from jax.sharding import PartitionSpec as P

ITERS = 3
EPSILON = 1e-06
SOFTMAX_WARMTH = 0.05
LANES = 128
HALF = 64
QUARTER = 32
SOFT_CHUNKS = 4
MESH = pl.DeviceIdType.MESH


def layout(dp_size):
    if dp_size == 256:
        return 4, 8, 8, 2, 2
    return 2, 2, dp_size // 4, 1, 1


def nearest_first(size):
    return sorted(range(size), key=lambda step: min(step, size - step))


def normalized_rows(values):
    return values * lax.rsqrt(jnp.mean(values * values, axis=-1, keepdims=True) + EPSILON)


def lane_sums(values):
    total = values[:, :LANES]
    for g in range(1, values.shape[1] // LANES):
        total = total + values[:, g * LANES : (g + 1) * LANES]
    return jnp.sum(total.T, axis=0, keepdims=True)


def fused(
    dims,
    tok_hbm,
    cen_hbm,
    new_ref,
    res_ref,
    tok_ref,
    cen_ref,
    toks,
    toks_t,
    cens,
    kern,
    tile_acc,
    rows_mine,
    rows_pair,
    rows_in,
    weights,
    weight_cols,
    cols_in,
    half_mat,
    sums_out,
    sums_in,
    news,
    soft,
    soft_pair,
    soft_half,
    soft_in,
    soft_fin,
    send_sem,
    recv_sem,
    load_sem,
):
    X, Y, Z, BY, BZ = dims
    AY, AZ = Y // BY, Z // BZ
    NB, NA = X * BY * BZ, AY * AZ
    rows_here = tok_ref.shape[0]
    load_tok = pltpu.make_async_copy(tok_hbm, tok_ref, load_sem.at[0])
    load_cen = pltpu.make_async_copy(cen_hbm, cen_ref, load_sem.at[1])
    load_tok.start()
    load_cen.start()
    panel = AZ * HALF
    groups = NA * HALF // LANES
    per_panel = panel // LANES
    many = min(NB, 4)
    col_mass = (rows_here * X * Y * Z) / (HALF * X * Y * Z * 2)

    dp = lax.axis_index("dp")
    core = lax.axis_index("cent")
    y = lax.rem(dp, Y)
    z = lax.rem(lax.div(dp, Y), Z)
    x = lax.div(dp, Y * Z)
    yb, ya = lax.rem(y, BY), lax.div(y, BY)
    zb, za = lax.rem(z, BZ), lax.div(z, BZ)
    sibling = (dp, 1 - core)

    def row_peer(r):
        px = lax.rem(x + r // (BY * BZ), X)
        py = lax.rem(yb + (r // BZ) % BY, BY)
        pz = lax.rem(zb + r % BZ, BZ)
        return (px * Z + za * BZ + pz) * Y + ya * BY + py, (px * BY + py) * BZ + pz

    def col_peer(r):
        py = lax.rem(ya + r // AZ, AY)
        pz = lax.rem(za + r % AZ, AZ)
        return (x * Z + pz * BZ + zb) * Y + py * BY + yb, py * AZ + pz

    row_peers = [row_peer(r) for r in range(NB)]
    col_peers = [col_peer(r) for r in range(NA)]
    mine_b = row_peers[0][1]
    mine_a = col_peers[0][1]
    row_ids = [(p[0], core) for p in row_peers]
    col_ids = [(p[0], core) for p in col_peers]
    steps = nearest_first(AY)
    panel_at = [lax.rem(ya + (AY - step) % AY, AY) for step in range(AY)]
    far_first = [step * AZ + other for step in reversed(steps) for other in reversed(nearest_first(AZ))]

    span = BY * BZ
    row_far = [step * span + other for step in reversed(nearest_first(X)) for other in reversed(range(span))]

    barrier = pltpu.get_barrier_semaphore()
    along_z = [r for r in nearest_first(AZ) if r]
    along_y = [step * AZ for step in steps if step]
    greeted = row_ids[1:] + [col_ids[r] for r in along_z + along_y] + [sibling]
    for peer in greeted:
        pl.semaphore_signal(barrier, inc=1, device_id=peer, device_id_type=MESH)

    def send(src, dst, phase, peer):
        pltpu.make_async_remote_copy(
            src_ref=src,
            dst_ref=dst,
            send_sem=send_sem.at[phase],
            recv_sem=recv_sem.at[phase],
            device_id=peer,
            device_id_type=MESH,
        ).start()

    sent = []

    def arrived(view, phase):
        pltpu.make_async_copy(view, view, recv_sem.at[phase]).wait()
        sent.append((view, phase))

    phases = iter(range(56))

    def slot(b):
        return jnp.concatenate([toks[0, b], toks[1, b]], axis=0)

    load_tok.wait()
    load_cen.wait()
    pad = jnp.zeros((LANES - rows_here, LANES), jnp.float32)
    unit_tok = jnp.concatenate([normalized_rows(tok_ref[...]), pad], axis=0)
    toks[core, mine_b] = jnp.where(core == 0, unit_tok[:HALF], unit_tok[HALF:]).astype(jnp.bfloat16)
    cens[mine_a] = normalized_rows(cen_ref[...]).astype(jnp.bfloat16)
    pl.semaphore_wait(barrier, len(greeted))
    tok_phase, pair_phase = next(phases), next(phases)
    z_phases = [next(phases) for _ in range(AZ)]
    y_phases = [next(phases) for _ in range(AY)]
    cen_phases = [next(phases) for _ in range(AY)]
    cross_phases = [next(phases) for _ in range(AY)]
    for r in reversed(along_z):
        send(cens.at[mine_a], cens.at[mine_a], z_phases[r], col_ids[r])
    for r in reversed(along_y):
        send(cens.at[mine_a], cens.at[mine_a], y_phases[r // AZ], col_ids[r])
    for r in row_far[:-1]:
        send(toks.at[core, mine_b], toks.at[core, mine_b], tok_phase, row_ids[r])
    low, high = pl.ds(0, QUARTER), pl.ds(QUARTER, QUARTER)
    for turn_of in range(max(AY, AZ) - 1):
        if turn_of < AZ - 1:
            step = along_z[turn_of]
            piece = ya * AZ + lax.rem(za + AZ - step, AZ)
            arrived(cens.at[0], z_phases[step])
            for r in reversed(along_y):
                send(cens.at[piece, low], cens.at[piece, low], cen_phases[r // AZ], col_ids[r])
        if turn_of < AY - 1:
            step = along_y[turn_of] // AZ
            piece = panel_at[step] * AZ + za
            arrived(cens.at[0], y_phases[step])
            for r in reversed(along_z):
                send(cens.at[piece, high], cens.at[piece, high], cross_phases[step], col_ids[r])
    arrived(toks.at[0, pl.ds(0, NB - 1)], tok_phase)
    send(toks.at[core], toks.at[core], pair_phase, sibling)
    arrived(toks.at[0], pair_phase)

    slope = math.log2(math.e) / (SOFTMAX_WARMTH * LANES)
    offset = math.log2(math.e) / SOFTMAX_WARMTH
    for order, step in enumerate(steps):
        at = panel_at[step]
        if step:
            arrived(cens.at[pl.ds(0, AZ - 1), low], cen_phases[step])
            arrived(cens.at[pl.ds(0, AZ - 1), high], cross_phases[step])
        columns = cens[pl.ds(at * AZ, AZ)].reshape(panel, LANES)

        def kernel_rows(i, carry):
            first = i * many
            block = jnp.concatenate([slot(first + j) for j in range(many)], axis=0)
            affinity = lax.dot_general(
                block, columns, (((1,), (1,)), ((), ())), preferred_element_type=jnp.float32
            )
            kernel = jnp.exp2(affinity * slope - offset)
            for j in range(many):
                part = kernel[j * LANES : (j + 1) * LANES]
                kern[at, first + j] = part
                total = part[:, :LANES]
                for h in range(1, per_panel):
                    total = total + part[:, h * LANES : (h + 1) * LANES]
                if order:
                    total = total + tile_acc[first + j]
                if order < AY - 1:
                    tile_acc[first + j] = total
                else:
                    rows_mine[0, pl.ds(first + j, 1), :] = jnp.sum(total.T, axis=0, keepdims=True)
            return carry

        lax.fori_loop(0, NB // many, kernel_rows, 0)

    def part_of(b, g):
        h = g % per_panel
        return kern[g // per_panel, b, :, h * LANES : (h + 1) * LANES]

    valid = lax.broadcasted_iota(jnp.int32, (NB, LANES), 1) < rows_here
    scales = None
    for it in range(ITERS):
        if it:
            scale_rows = scales

            def scaled_rows(b, carry):
                total = part_of(b, 0) * scale_rows[0:1, :]
                for g in range(1, groups):
                    total = total + part_of(b, g) * scale_rows[g : g + 1, :]
                rows_mine[it, pl.ds(b, 1), :] = jnp.sum(total.T, axis=0, keepdims=True)
                return carry

            lax.fori_loop(0, NB, scaled_rows, 0, unroll=many)

        phase = next(phases)
        send(rows_mine.at[it], rows_pair.at[it], phase, sibling)
        arrived(rows_pair.at[it], phase)
        rows_in[it, 0] = rows_mine[it] + rows_pair[it]
        phase = next(phases)
        for r in row_far[:-1]:
            send(rows_in.at[it, 0], rows_in.at[it, r], phase, row_ids[r])
        if it == 0:
            def turn(b, carry):
                place = pl.ds(pl.multiple_of(b * LANES, LANES), LANES)
                toks_t[:, place] = slot(b).astype(jnp.float32).T.astype(jnp.bfloat16)
                return carry

            lax.fori_loop(0, NB, turn, 0, unroll=many)
        arrived(rows_in.at[it, pl.ds(1, NB - 1)], phase)
        row_sum = jnp.sum(rows_in[it], axis=0)
        weights[...] = jnp.where(valid, 1.0 / row_sum, 0.0)

        def weighted_columns(b, totals):
            spread = jnp.broadcast_to(weights[pl.ds(b, 1), :], (LANES, LANES)).T
            weight_cols[b] = spread
            return tuple(
                totals[g] + jnp.sum((part_of(b, g) * spread).reshape(LANES // 8, 8, LANES), axis=0)
                for g in range(groups)
            )

        zeros = tuple(jnp.zeros((8, LANES), jnp.float32) for _ in range(groups))
        totals = lax.fori_loop(0, NB, weighted_columns, zeros, unroll=many)
        for g in range(groups):
            cols_in[it, 0, g : g + 1, :] = jnp.sum(totals[g], axis=0, keepdims=True)
        col_phase = next(phases)
        for r in far_first:
            if r:
                send(cols_in.at[it, 0], cols_in.at[it, r], col_phase, col_ids[r])

        if it == ITERS - 1:
            sums_phases = next(phases), next(phases)

            def send_sums(half, peers):
                for r in peers:
                    part = sums_out.at[col_peers[r][1], pl.ds(half * QUARTER, QUARTER)]
                    send(part, sums_in.at[half, r], sums_phases[half], col_ids[r])

            for step in reversed(steps):
                at = lax.rem(ya + step, AY)

                def assign_rows(b, carry):
                    spread = weight_cols[b].astype(jnp.bfloat16).astype(jnp.float32)
                    for h in range(per_panel):
                        lanes = slice(h * LANES, (h + 1) * LANES)
                        half_mat[step, b, :, lanes] = (kern[at, b, :, lanes] * spread).astype(jnp.bfloat16)
                    return carry

                lax.fori_loop(0, NB, assign_rows, 0, unroll=many)
                turned = jnp.dot(
                    toks_t[...],
                    half_mat[step].reshape(NB * LANES, panel),
                    preferred_element_type=jnp.float32,
                )
                for h in range(per_panel):
                    pair = turned[:, h * LANES : (h + 1) * LANES].T
                    sums_out[at * AZ + 2 * h] = pair[:HALF]
                    sums_out[at * AZ + 2 * h + 1] = pair[HALF:]
                send_sums(0, [r for r in far_first if r and r // AZ == step])
            send_sums(1, far_first[:-1])
            for half in range(2):
                sums_in[half, 0] = sums_out[mine_a, half * QUARTER : (half + 1) * QUARTER]

        arrived(cols_in.at[it, pl.ds(1, NA - 1)], col_phase)
        scales = col_mass / jnp.sum(cols_in[it], axis=0)

    last_scales = scales

    def plan_rows(b, carry):
        spread = weight_cols[b]
        for g in range(groups):
            h = g % per_panel
            half_mat[g // per_panel, b, :, h * LANES : (h + 1) * LANES] = (
                part_of(b, g) * spread * last_scales[g : g + 1, :]
            ).astype(jnp.bfloat16)
        return carry

    lax.fori_loop(0, NB, plan_rows, 0, unroll=many)

    new_phases = [next(phases) for _ in range(AY)]
    for half in range(2):
        arrived(sums_in.at[half, pl.ds(1, NA - 1)], sums_phases[half])
        new_own = normalized_rows(jnp.sum(sums_in[half], axis=0))
        place = pl.ds(half * QUARTER, QUARTER)
        news[mine_a, place] = new_own.astype(jnp.bfloat16)
        for r in far_first[:-1]:
            send(news.at[mine_a, place], news.at[mine_a, place], new_phases[r // AZ], col_ids[r])
        new_ref[place, :] = new_own

    chunk = max(NB // SOFT_CHUNKS, 1)
    soft_phases = []
    firsts = [step * chunk for step in reversed(nearest_first(NB // chunk))]
    for order, step in enumerate(steps):
        at = panel_at[step]
        arrived(news.at[pl.ds(0, AZ - (step == 0))], new_phases[step])
        fresh = news[pl.ds(at * AZ, AZ)].reshape(panel, LANES)
        if order < AY - 1:

            def soft_rows(i, carry):
                place = pl.ds(i * many, many)
                block = jnp.dot(
                    half_mat[at, place].reshape(many * LANES, panel), fresh, preferred_element_type=jnp.float32
                ).reshape(many, LANES, LANES)
                tile_acc[place] = block if order == 0 else tile_acc[place] + block
                return carry

            lax.fori_loop(0, NB // many, soft_rows, 0)
            continue
        for first in firsts:
            block = jnp.dot(
                jnp.concatenate([half_mat[at, row_peers[r][1]] for r in range(first, first + chunk)], axis=0),
                fresh,
                preferred_element_type=jnp.float32,
            )
            for r in range(first, first + chunk):
                whole = block[(r - first) * LANES : (r - first + 1) * LANES] + tile_acc[row_peers[r][1]]
                soft[0, r] = whole[:HALF]
                soft[1, r] = whole[HALF:]
            phase = next(phases)
            soft_phases.append(phase)
            send(soft.at[1 - core, pl.ds(first, chunk)], soft_pair.at[pl.ds(first, chunk)], phase, sibling)
    soft_phase = next(phases)
    for first, phase in zip(firsts, soft_phases):
        arrived(soft_pair.at[pl.ds(first, chunk)], phase)
        for r in reversed(range(first, first + chunk)):
            if r == 0:
                soft_in[0] = soft[core, 0] + soft_pair[0]
            else:
                soft_half[r] = soft[core, r] + soft_pair[r]
                send(soft_half.at[r], soft_in.at[r], soft_phase, row_ids[r])
    arrived(soft_in.at[pl.ds(1, NB - 1)], soft_phase)
    soft_fin[core] = jnp.sum(soft_in[...], axis=0)
    phase = next(phases)
    send(soft_fin.at[core], soft_fin.at[core], phase, sibling)
    unit_tok = normalized_rows(tok_ref[...])
    arrived(soft_fin.at[0], phase)
    whole = jnp.concatenate([soft_fin[0], soft_fin[1]], axis=0)
    res_ref[...] = unit_tok - whole[:rows_here, :]
    for view, used in sent:
        pltpu.make_async_copy(view, view, send_sem.at[used]).wait()


def shards(dims, tokens, centroids):
    X, Y, Z, BY, BZ = dims
    AY, AZ = Y // BY, Z // BZ
    NB, NA = X * BY * BZ, AY * AZ
    panel = AZ * HALF
    groups = NA * HALF // LANES
    f32, bf16 = jnp.float32, jnp.bfloat16
    scratch = [
        pltpu.VMEM(tokens.shape, f32),
        pltpu.VMEM(centroids.shape, f32),
        pltpu.VMEM((2, NB, HALF, LANES), bf16),
        pltpu.VMEM((LANES, NB * LANES), bf16),
        pltpu.VMEM((NA, HALF, LANES), bf16),
        pltpu.VMEM((AY, NB, LANES, panel), f32),
        pltpu.VMEM((NB, LANES, LANES), f32),
        pltpu.VMEM((ITERS, NB, LANES), f32),
        pltpu.VMEM((ITERS, NB, LANES), f32),
        pltpu.VMEM((ITERS, NB, NB, LANES), f32),
        pltpu.VMEM((NB, LANES), f32),
        pltpu.VMEM((NB, LANES, LANES), f32),
        pltpu.VMEM((ITERS, NA, groups, LANES), f32),
        pltpu.VMEM((AY, NB, LANES, panel), bf16),
        pltpu.VMEM((NA, HALF, LANES), f32),
        pltpu.VMEM((2, NA, QUARTER, LANES), f32),
        pltpu.VMEM((NA, HALF, LANES), bf16),
        pltpu.VMEM((2, NB, HALF, LANES), f32),
        pltpu.VMEM((NB, HALF, LANES), f32),
        pltpu.VMEM((NB, HALF, LANES), f32),
        pltpu.VMEM((NB, HALF, LANES), f32),
        pltpu.VMEM((2, HALF, LANES), f32),
        pltpu.SemaphoreType.DMA((56,)),
        pltpu.SemaphoreType.DMA((56,)),
        pltpu.SemaphoreType.DMA((2,)),
    ]
    return pl.pallas_call(
        functools.partial(fused, dims),
        out_shape=(
            jax.ShapeDtypeStruct(centroids.shape, f32),
            jax.ShapeDtypeStruct(tokens.shape, f32),
        ),
        in_specs=[pl.BlockSpec(memory_space=pl.ANY)] * 2,
        out_specs=[pl.BlockSpec(memory_space=pltpu.VMEM)] * 2,
        scratch_shapes=scratch,
        compiler_params=pltpu.CompilerParams(
            collective_id=0, has_side_effects=True, vmem_limit_bytes=48 * 1024 * 1024
        ),
        name="kmeans_step",
    )(tokens, centroids)


def solution(mesh):
    in_specs = (P("dp", None), P(("dp", "cent"), None))
    out_specs = (P(("dp", "cent"), None), P("dp", None))
    dims = layout(mesh.shape["dp"])
    return jax.shard_map(
        functools.partial(shards, dims), mesh=mesh, in_specs=in_specs, out_specs=out_specs, check_vma=False
    )
```

```python
import functools
import math

import jax
import jax.numpy as jnp
from jax import lax
from jax.experimental import pallas as pl
from jax.experimental.pallas import tpu as pltpu
from jax.sharding import PartitionSpec as P

ITERS = 3
EPSILON = 1e-06
SOFTMAX_WARMTH = 0.05
LANES = 128
HALF = 64
QUARTER = 32
PART = 16
PARTS = HALF // PART
SOFT_CHUNKS = 4
MESH = pl.DeviceIdType.MESH


def layout(dp_size):
    if dp_size == 256:
        return 4, 8, 8, 2, 2
    return 2, 2, dp_size // 4, 1, 1


def nearest_first(size):
    return sorted(range(size), key=lambda step: min(step, size - step))


def normalized_rows(values):
    return values * lax.rsqrt(jnp.mean(values * values, axis=-1, keepdims=True) + EPSILON)


def lane_sums(values):
    total = values[:, :LANES]
    for g in range(1, values.shape[1] // LANES):
        total = total + values[:, g * LANES : (g + 1) * LANES]
    return jnp.sum(total.T, axis=0, keepdims=True)


def fused(
    dims,
    tok_hbm,
    cen_hbm,
    new_ref,
    res_ref,
    tok_ref,
    cen_ref,
    toks,
    toks_t,
    cens,
    kern,
    tile_acc,
    rows_mine,
    rows_pair,
    rows_in,
    weights,
    weight_cols,
    cols_in,
    half_mat,
    sums_out,
    sums_in,
    news,
    soft,
    soft_pair,
    soft_half,
    soft_in,
    soft_fin,
    send_sem,
    recv_sem,
    load_sem,
):
    X, Y, Z, BY, BZ = dims
    AY, AZ = Y // BY, Z // BZ
    NB, NA = X * BY * BZ, AY * AZ
    rows_here = tok_ref.shape[0]
    load_tok = pltpu.make_async_copy(tok_hbm, tok_ref, load_sem.at[0])
    load_cen = pltpu.make_async_copy(cen_hbm, cen_ref, load_sem.at[1])
    load_tok.start()
    load_cen.start()
    panel = AZ * HALF
    groups = NA * HALF // LANES
    per_panel = panel // LANES
    side = NB // 2
    many = min(side, 4)
    col_mass = (rows_here * X * Y * Z) / (HALF * X * Y * Z * 2)

    dp = lax.axis_index("dp")
    core = lax.axis_index("cent")
    y = lax.rem(dp, Y)
    z = lax.rem(lax.div(dp, Y), Z)
    x = lax.div(dp, Y * Z)
    yb, ya = lax.rem(y, BY), lax.div(y, BY)
    zb, za = lax.rem(z, BZ), lax.div(z, BZ)
    sibling = (dp, 1 - core)

    def row_peer(r):
        px = lax.rem(x + r // (BY * BZ), X)
        py = lax.rem(yb + (r // BZ) % BY, BY)
        pz = lax.rem(zb + r % BZ, BZ)
        return (px * Z + za * BZ + pz) * Y + ya * BY + py, (px * BY + py) * BZ + pz

    def col_peer(r):
        py = lax.rem(ya + r // AZ, AY)
        pz = lax.rem(za + r % AZ, AZ)
        return (x * Z + pz * BZ + zb) * Y + py * BY + yb, py * AZ + pz

    row_peers = [row_peer(r) for r in range(NB)]
    col_peers = [col_peer(r) for r in range(NA)]
    mine_b = row_peers[0][1]
    mine_a = col_peers[0][1]
    row_ids = [(p[0], core) for p in row_peers]
    col_ids = [(p[0], core) for p in col_peers]
    steps = nearest_first(AY)
    panel_at = [lax.rem(ya + (AY - step) % AY, AY) for step in range(AY)]
    far_first = [step * AZ + other for step in reversed(steps) for other in reversed(nearest_first(AZ))]

    span = BY * BZ
    row_far = [step * span + other for step in reversed(nearest_first(X)) for other in reversed(range(span))]

    barrier = pltpu.get_barrier_semaphore()
    along_z = [r for r in nearest_first(AZ) if r]
    along_y = [step * AZ for step in steps if step]
    greeted = row_ids[1:] + [col_ids[r] for r in along_z + along_y] + [sibling]
    for peer in greeted:
        pl.semaphore_signal(barrier, inc=1, device_id=peer, device_id_type=MESH)

    def send(src, dst, phase, peer):
        pltpu.make_async_remote_copy(
            src_ref=src,
            dst_ref=dst,
            send_sem=send_sem.at[phase],
            recv_sem=recv_sem.at[phase],
            device_id=peer,
            device_id_type=MESH,
        ).start()

    sent = []

    def arrived(view, phase):
        pltpu.make_async_copy(view, view, recv_sem.at[phase]).wait()
        sent.append((view, phase))

    phases = iter(range(64))

    def slot(b):
        return jnp.concatenate([toks[0, b], toks[1, b]], axis=0)

    load_tok.wait()
    load_cen.wait()
    pad = jnp.zeros((LANES - rows_here, LANES), jnp.float32)
    unit_tok = jnp.concatenate([normalized_rows(tok_ref[...]), pad], axis=0)
    toks[core, mine_b] = jnp.where(core == 0, unit_tok[:HALF], unit_tok[HALF:]).astype(jnp.bfloat16)
    cens[mine_a] = normalized_rows(cen_ref[...]).astype(jnp.bfloat16)
    pl.semaphore_wait(barrier, len(greeted))
    tok_phase, pair_phase = next(phases), next(phases)
    z_phases = [next(phases) for _ in range(AZ)]
    y_phases = [next(phases) for _ in range(AY)]
    cen_phases = [next(phases) for _ in range(AY)]
    cross_phases = [next(phases) for _ in range(AY)]
    for r in reversed(along_z):
        send(cens.at[mine_a], cens.at[mine_a], z_phases[r], col_ids[r])
    for r in reversed(along_y):
        send(cens.at[mine_a], cens.at[mine_a], y_phases[r // AZ], col_ids[r])
    for r in row_far[:-1]:
        send(toks.at[core, mine_b], toks.at[core, mine_b], tok_phase, row_ids[r])
    low, high = pl.ds(0, QUARTER), pl.ds(QUARTER, QUARTER)
    for turn_of in range(max(AY, AZ) - 1):
        if turn_of < AZ - 1:
            step = along_z[turn_of]
            piece = ya * AZ + lax.rem(za + AZ - step, AZ)
            arrived(cens.at[0], z_phases[step])
            for r in reversed(along_y):
                send(cens.at[piece, low], cens.at[piece, low], cen_phases[r // AZ], col_ids[r])
        if turn_of < AY - 1:
            step = along_y[turn_of] // AZ
            piece = panel_at[step] * AZ + za
            arrived(cens.at[0], y_phases[step])
            for r in reversed(along_z):
                send(cens.at[piece, high], cens.at[piece, high], cross_phases[step], col_ids[r])
    arrived(toks.at[0, pl.ds(0, NB - 1)], tok_phase)
    send(toks.at[core], toks.at[core], pair_phase, sibling)
    arrived(toks.at[0], pair_phase)

    pair_rows_phases = []

    def pair_rows(it, half):
        view = pl.ds(half * side, side)
        pair_rows_phases.append(next(phases))
        send(rows_mine.at[it, view], rows_pair.at[it, view], pair_rows_phases[-1], sibling)

    slope = math.log2(math.e) / (SOFTMAX_WARMTH * LANES)
    offset = math.log2(math.e) / SOFTMAX_WARMTH
    for order, step in enumerate(steps):
        at = panel_at[step]
        if step:
            arrived(cens.at[pl.ds(0, AZ - 1), low], cen_phases[step])
            arrived(cens.at[pl.ds(0, AZ - 1), high], cross_phases[step])
        columns = cens[pl.ds(at * AZ, AZ)].reshape(panel, LANES)

        def kernel_rows(i, carry):
            first = i * many
            block = jnp.concatenate([slot(first + j) for j in range(many)], axis=0)
            affinity = lax.dot_general(
                block, columns, (((1,), (1,)), ((), ())), preferred_element_type=jnp.float32
            )
            kernel = jnp.exp2(affinity * slope - offset)
            for j in range(many):
                part = kernel[j * LANES : (j + 1) * LANES]
                kern[at, first + j] = part
                total = part[:, :LANES]
                for h in range(1, per_panel):
                    total = total + part[:, h * LANES : (h + 1) * LANES]
                if order:
                    total = total + tile_acc[first + j]
                if order < AY - 1:
                    tile_acc[first + j] = total
                else:
                    rows_mine[0, pl.ds(first + j, 1), :] = jnp.sum(total.T, axis=0, keepdims=True)
            return carry

        lax.fori_loop(0, side // many, kernel_rows, 0)
        if order == AY - 1:
            pair_rows(0, 0)
        lax.fori_loop(side // many, NB // many, kernel_rows, 0)
        if order == AY - 1:
            pair_rows(0, 1)

    def part_of(b, g):
        h = g % per_panel
        return kern[g // per_panel, b, :, h * LANES : (h + 1) * LANES]

    valid = lax.broadcasted_iota(jnp.int32, (side, LANES), 1) < rows_here
    scales = None
    for it in range(ITERS):
        if it:
            scale_rows = scales

            def scaled_rows(b, carry):
                total = part_of(b, 0) * scale_rows[0:1, :]
                for g in range(1, groups):
                    total = total + part_of(b, g) * scale_rows[g : g + 1, :]
                rows_mine[it, pl.ds(b, 1), :] = jnp.sum(total.T, axis=0, keepdims=True)
                return carry

            for half in range(2):
                lax.fori_loop(half * side, half * side + side, scaled_rows, 0, unroll=many)
                pair_rows(it, half)

        rows_phases = next(phases), next(phases)
        for half in range(2):
            view = pl.ds(half * side, side)
            arrived(rows_pair.at[it, view], pair_rows_phases[2 * it + half])
            rows_in[it, half, 0] = rows_mine[it, view] + rows_pair[it, view]
            for r in row_far[:-1]:
                send(rows_in.at[it, half, 0], rows_in.at[it, half, r], rows_phases[half], row_ids[r])
        if it == 0:
            def turn(b, carry):
                place = pl.ds(pl.multiple_of(b * LANES, LANES), LANES)
                toks_t[:, place] = slot(b).astype(jnp.float32).T.astype(jnp.bfloat16)
                return carry

            lax.fori_loop(0, NB, turn, 0, unroll=many)
        def weighted_columns(b, totals):
            spread = jnp.broadcast_to(weights[pl.ds(b, 1), :], (LANES, LANES)).T
            weight_cols[b] = spread
            return tuple(
                totals[g] + jnp.sum((part_of(b, g) * spread).reshape(LANES // 8, 8, LANES), axis=0)
                for g in range(groups)
            )

        zeros = tuple(jnp.zeros((8, LANES), jnp.float32) for _ in range(groups))
        totals = zeros
        for half in range(2):
            arrived(rows_in.at[it, half, pl.ds(1, NB - 1)], rows_phases[half])
            row_sum = jnp.sum(rows_in[it, half], axis=0)
            weights[pl.ds(half * side, side), :] = jnp.where(valid, 1.0 / row_sum, 0.0)
            totals = lax.fori_loop(half * side, half * side + side, weighted_columns, totals, unroll=many)
        for g in range(groups):
            cols_in[it, 0, g : g + 1, :] = jnp.sum(totals[g], axis=0, keepdims=True)
        col_phase = next(phases)
        for r in far_first:
            if r:
                send(cols_in.at[it, 0], cols_in.at[it, r], col_phase, col_ids[r])

        if it == ITERS - 1:
            sums_phases = [next(phases) for _ in range(PARTS)]

            def send_sums(half, peers):
                for r in peers:
                    part = sums_out.at[col_peers[r][1], pl.ds(half * PART, PART)]
                    send(part, sums_in.at[half, r], sums_phases[half], col_ids[r])

            for step in reversed(steps):
                at = lax.rem(ya + step, AY)

                def assign_rows(b, carry):
                    spread = weight_cols[b].astype(jnp.bfloat16).astype(jnp.float32)
                    for h in range(per_panel):
                        lanes = slice(h * LANES, (h + 1) * LANES)
                        half_mat[step, b, :, lanes] = (kern[at, b, :, lanes] * spread).astype(jnp.bfloat16)
                    return carry

                lax.fori_loop(0, NB, assign_rows, 0, unroll=many)
                turned = jnp.dot(
                    toks_t[...],
                    half_mat[step].reshape(NB * LANES, panel),
                    preferred_element_type=jnp.float32,
                )
                for h in range(per_panel):
                    pair = turned[:, h * LANES : (h + 1) * LANES].T
                    sums_out[at * AZ + 2 * h] = pair[:HALF]
                    sums_out[at * AZ + 2 * h + 1] = pair[HALF:]
                send_sums(0, [r for r in far_first if r and r // AZ == step])
            for half in range(1, PARTS):
                send_sums(half, far_first[:-1])
            for half in range(PARTS):
                sums_in[half, 0] = sums_out[mine_a, half * PART : (half + 1) * PART]

        arrived(cols_in.at[it, pl.ds(1, NA - 1)], col_phase)
        scales = col_mass / jnp.sum(cols_in[it], axis=0)

    last_scales = scales

    def plan_rows(b, carry):
        spread = weight_cols[b]
        for g in range(groups):
            h = g % per_panel
            half_mat[g // per_panel, b, :, h * LANES : (h + 1) * LANES] = (
                part_of(b, g) * spread * last_scales[g : g + 1, :]
            ).astype(jnp.bfloat16)
        return carry

    lax.fori_loop(0, NB, plan_rows, 0, unroll=many)

    new_phases = [next(phases) for _ in range(AY)]
    for half in range(PARTS):
        arrived(sums_in.at[half, pl.ds(1, NA - 1)], sums_phases[half])
        new_own = normalized_rows(jnp.sum(sums_in[half], axis=0))
        place = pl.ds(half * PART, PART)
        news[mine_a, place] = new_own.astype(jnp.bfloat16)
        for r in far_first[:-1]:
            send(news.at[mine_a, place], news.at[mine_a, place], new_phases[r // AZ], col_ids[r])
        new_ref[place, :] = new_own

    chunk = max(NB // SOFT_CHUNKS, 1)
    soft_phases = []
    firsts = [step * chunk for step in reversed(nearest_first(NB // chunk))]
    for order, step in enumerate(steps):
        at = panel_at[step]
        arrived(news.at[pl.ds(0, AZ - (step == 0))], new_phases[step])
        fresh = news[pl.ds(at * AZ, AZ)].reshape(panel, LANES)
        if order < AY - 1:

            def soft_rows(i, carry):
                place = pl.ds(i * many, many)
                block = jnp.dot(
                    half_mat[at, place].reshape(many * LANES, panel), fresh, preferred_element_type=jnp.float32
                ).reshape(many, LANES, LANES)
                tile_acc[place] = block if order == 0 else tile_acc[place] + block
                return carry

            lax.fori_loop(0, NB // many, soft_rows, 0)
            continue
        soft_phase = next(phases)

        def pass_on(first, phase):
            arrived(soft_pair.at[pl.ds(first, chunk)], phase)
            for r in reversed(range(first, first + chunk)):
                if r == 0:
                    soft_in[0] = soft[core, 0] + soft_pair[0]
                else:
                    soft_half[r] = soft[core, r] + soft_pair[r]
                    send(soft_half.at[r], soft_in.at[r], soft_phase, row_ids[r])

        for first in firsts:
            block = jnp.dot(
                jnp.concatenate([half_mat[at, row_peers[r][1]] for r in range(first, first + chunk)], axis=0),
                fresh,
                preferred_element_type=jnp.float32,
            )
            for r in range(first, first + chunk):
                whole = block[(r - first) * LANES : (r - first + 1) * LANES] + tile_acc[row_peers[r][1]]
                soft[0, r] = whole[:HALF]
                soft[1, r] = whole[HALF:]
            soft_phases.append((first, next(phases)))
            send(
                soft.at[1 - core, pl.ds(first, chunk)],
                soft_pair.at[pl.ds(first, chunk)],
                soft_phases[-1][1],
                sibling,
            )
            if len(soft_phases) > 1:
                pass_on(*soft_phases[-2])
        pass_on(*soft_phases[-1])
    arrived(soft_in.at[pl.ds(1, NB - 1)], soft_phase)
    soft_fin[core] = jnp.sum(soft_in[...], axis=0)
    phase = next(phases)
    send(soft_fin.at[core], soft_fin.at[core], phase, sibling)
    unit_tok = normalized_rows(tok_ref[...])
    arrived(soft_fin.at[0], phase)
    whole = jnp.concatenate([soft_fin[0], soft_fin[1]], axis=0)
    res_ref[...] = unit_tok - whole[:rows_here, :]
    for view, used in sent:
        pltpu.make_async_copy(view, view, send_sem.at[used]).wait()


def shards(dims, tokens, centroids):
    X, Y, Z, BY, BZ = dims
    AY, AZ = Y // BY, Z // BZ
    NB, NA = X * BY * BZ, AY * AZ
    panel = AZ * HALF
    groups = NA * HALF // LANES
    f32, bf16 = jnp.float32, jnp.bfloat16
    scratch = [
        pltpu.VMEM(tokens.shape, f32),
        pltpu.VMEM(centroids.shape, f32),
        pltpu.VMEM((2, NB, HALF, LANES), bf16),
        pltpu.VMEM((LANES, NB * LANES), bf16),
        pltpu.VMEM((NA, HALF, LANES), bf16),
        pltpu.VMEM((AY, NB, LANES, panel), f32),
        pltpu.VMEM((NB, LANES, LANES), f32),
        pltpu.VMEM((ITERS, NB, LANES), f32),
        pltpu.VMEM((ITERS, NB, LANES), f32),
        pltpu.VMEM((ITERS, 2, NB, NB // 2, LANES), f32),
        pltpu.VMEM((NB, LANES), f32),
        pltpu.VMEM((NB, LANES, LANES), f32),
        pltpu.VMEM((ITERS, NA, groups, LANES), f32),
        pltpu.VMEM((AY, NB, LANES, panel), bf16),
        pltpu.VMEM((NA, HALF, LANES), f32),
        pltpu.VMEM((PARTS, NA, PART, LANES), f32),
        pltpu.VMEM((NA, HALF, LANES), bf16),
        pltpu.VMEM((2, NB, HALF, LANES), f32),
        pltpu.VMEM((NB, HALF, LANES), f32),
        pltpu.VMEM((NB, HALF, LANES), f32),
        pltpu.VMEM((NB, HALF, LANES), f32),
        pltpu.VMEM((2, HALF, LANES), f32),
        pltpu.SemaphoreType.DMA((64,)),
        pltpu.SemaphoreType.DMA((64,)),
        pltpu.SemaphoreType.DMA((2,)),
    ]
    return pl.pallas_call(
        functools.partial(fused, dims),
        out_shape=(
            jax.ShapeDtypeStruct(centroids.shape, f32),
            jax.ShapeDtypeStruct(tokens.shape, f32),
        ),
        in_specs=[pl.BlockSpec(memory_space=pl.ANY)] * 2,
        out_specs=[pl.BlockSpec(memory_space=pltpu.VMEM)] * 2,
        scratch_shapes=scratch,
        compiler_params=pltpu.CompilerParams(
            collective_id=0, has_side_effects=True, vmem_limit_bytes=48 * 1024 * 1024
        ),
        name="kmeans_step",
    )(tokens, centroids)


def solution(mesh):
    in_specs = (P("dp", None), P(("dp", "cent"), None))
    out_specs = (P(("dp", "cent"), None), P("dp", None))
    dims = layout(mesh.shape["dp"])
    return jax.shard_map(
        functools.partial(shards, dims), mesh=mesh, in_specs=in_specs, out_specs=out_specs, check_vma=False
    )
```

```python
import functools
import math

import jax
import jax.numpy as jnp
from jax import lax
from jax.experimental import pallas as pl
from jax.experimental.pallas import tpu as pltpu
from jax.sharding import PartitionSpec as P

ITERS = 3
EPSILON = 1e-06
SOFTMAX_WARMTH = 0.05
LANES = 128
HALF = 64
QUARTER = 32
PART = 16
PARTS = HALF // PART
SOFT_CHUNKS = 4
MESH = pl.DeviceIdType.MESH


def layout(dp_size):
    if dp_size == 256:
        return 4, 8, 8, 2, 2
    return 2, 2, dp_size // 4, 1, 1


def nearest_first(size):
    return sorted(range(size), key=lambda step: min(step, size - step))


def normalized_rows(values):
    return values * lax.rsqrt(jnp.mean(values * values, axis=-1, keepdims=True) + EPSILON)


def lane_sums(values):
    total = values[:, :LANES]
    for g in range(1, values.shape[1] // LANES):
        total = total + values[:, g * LANES : (g + 1) * LANES]
    return jnp.sum(total.T, axis=0, keepdims=True)


def fused(
    dims,
    tok_hbm,
    cen_hbm,
    new_ref,
    res_ref,
    tok_ref,
    cen_ref,
    toks,
    toks_t,
    cens,
    kern,
    tile_acc,
    rows_mine,
    rows_pair,
    rows_in,
    weights,
    weight_cols,
    cols_in,
    half_mat,
    sums_out,
    sums_in,
    news,
    soft,
    soft_pair,
    soft_half,
    soft_in,
    soft_fin,
    send_sem,
    recv_sem,
    load_sem,
):
    X, Y, Z, BY, BZ = dims
    AY, AZ = Y // BY, Z // BZ
    NB, NA = X * BY * BZ, AY * AZ
    rows_here = tok_ref.shape[0]
    load_tok = pltpu.make_async_copy(tok_hbm, tok_ref, load_sem.at[0])
    load_cen = pltpu.make_async_copy(cen_hbm, cen_ref, load_sem.at[1])
    load_tok.start()
    load_cen.start()
    panel = AZ * HALF
    groups = NA * HALF // LANES
    per_panel = panel // LANES
    side = NB // 2
    many = min(side, 4)
    col_mass = (rows_here * X * Y * Z) / (HALF * X * Y * Z * 2)

    dp = lax.axis_index("dp")
    core = lax.axis_index("cent")
    y = lax.rem(dp, Y)
    z = lax.rem(lax.div(dp, Y), Z)
    x = lax.div(dp, Y * Z)
    yb, ya = lax.rem(y, BY), lax.div(y, BY)
    zb, za = lax.rem(z, BZ), lax.div(z, BZ)
    sibling = (dp, 1 - core)

    def row_peer(r):
        px = lax.rem(x + r // (BY * BZ), X)
        py = lax.rem(yb + (r // BZ) % BY, BY)
        pz = lax.rem(zb + r % BZ, BZ)
        return (px * Z + za * BZ + pz) * Y + ya * BY + py, (px * BY + py) * BZ + pz

    def col_peer(r):
        py = lax.rem(ya + r // AZ, AY)
        pz = lax.rem(za + r % AZ, AZ)
        return (x * Z + pz * BZ + zb) * Y + py * BY + yb, py * AZ + pz

    row_peers = [row_peer(r) for r in range(NB)]
    col_peers = [col_peer(r) for r in range(NA)]
    mine_b = row_peers[0][1]
    mine_a = col_peers[0][1]
    row_ids = [(p[0], core) for p in row_peers]
    col_ids = [(p[0], core) for p in col_peers]
    steps = nearest_first(AY)
    panel_at = [lax.rem(ya + (AY - step) % AY, AY) for step in range(AY)]
    far_first = [step * AZ + other for step in reversed(steps) for other in reversed(nearest_first(AZ))]

    span = BY * BZ
    row_far = [step * span + other for step in reversed(nearest_first(X)) for other in reversed(range(span))]

    barrier = pltpu.get_barrier_semaphore()
    along_z = [r for r in nearest_first(AZ) if r]
    along_y = [step * AZ for step in steps if step]
    greeted = row_ids[1:] + [col_ids[r] for r in along_z + along_y] + [sibling]
    for peer in greeted:
        pl.semaphore_signal(barrier, inc=1, device_id=peer, device_id_type=MESH)

    def send(src, dst, phase, peer):
        pltpu.make_async_remote_copy(
            src_ref=src,
            dst_ref=dst,
            send_sem=send_sem.at[phase],
            recv_sem=recv_sem.at[phase],
            device_id=peer,
            device_id_type=MESH,
        ).start()

    sent = []

    def arrived(view, phase):
        pltpu.make_async_copy(view, view, recv_sem.at[phase]).wait()
        sent.append((view, phase))

    phases = iter(range(64))

    def slot(b):
        return jnp.concatenate([toks[0, b], toks[1, b]], axis=0)

    load_tok.wait()
    load_cen.wait()
    pad = jnp.zeros((LANES - rows_here, LANES), jnp.float32)
    unit_tok = jnp.concatenate([normalized_rows(tok_ref[...]), pad], axis=0)
    toks[core, mine_b] = jnp.where(core == 0, unit_tok[:HALF], unit_tok[HALF:]).astype(jnp.bfloat16)
    cens[mine_a] = normalized_rows(cen_ref[...]).astype(jnp.bfloat16)
    pl.semaphore_wait(barrier, len(greeted))
    tok_phase, pair_phase = next(phases), next(phases)
    z_phases = [next(phases) for _ in range(AZ)]
    y_phases = [next(phases) for _ in range(AY)]
    cen_phases = [next(phases) for _ in range(AY)]
    cross_phases = [next(phases) for _ in range(AY)]
    for r in reversed(along_z):
        send(cens.at[mine_a], cens.at[mine_a], z_phases[r], col_ids[r])
    for r in reversed(along_y):
        send(cens.at[mine_a], cens.at[mine_a], y_phases[r // AZ], col_ids[r])
    for r in row_far[:-1]:
        send(toks.at[core, mine_b], toks.at[core, mine_b], tok_phase, row_ids[r])
    low, high = pl.ds(0, QUARTER), pl.ds(QUARTER, QUARTER)
    for turn_of in range(max(AY, AZ) - 1):
        if turn_of < AZ - 1:
            step = along_z[turn_of]
            piece = ya * AZ + lax.rem(za + AZ - step, AZ)
            arrived(cens.at[0], z_phases[step])
            for r in reversed(along_y):
                send(cens.at[piece, low], cens.at[piece, low], cen_phases[r // AZ], col_ids[r])
        if turn_of < AY - 1:
            step = along_y[turn_of] // AZ
            piece = panel_at[step] * AZ + za
            arrived(cens.at[0], y_phases[step])
            for r in reversed(along_z):
                send(cens.at[piece, high], cens.at[piece, high], cross_phases[step], col_ids[r])
    arrived(toks.at[0, pl.ds(0, NB - 1)], tok_phase)
    send(toks.at[core], toks.at[core], pair_phase, sibling)
    arrived(toks.at[0], pair_phase)

    pair_rows_phases = []

    def pair_rows(it, half):
        view = pl.ds(half * side, side)
        pair_rows_phases.append(next(phases))
        send(rows_mine.at[it, view], rows_pair.at[it, view], pair_rows_phases[-1], sibling)

    slope = math.log2(math.e) / (SOFTMAX_WARMTH * LANES)
    offset = math.log2(math.e) / SOFTMAX_WARMTH
    for order, step in enumerate(steps):
        at = panel_at[step]
        if step:
            arrived(cens.at[pl.ds(0, AZ - 1), low], cen_phases[step])
            arrived(cens.at[pl.ds(0, AZ - 1), high], cross_phases[step])
        columns = cens[pl.ds(at * AZ, AZ)].reshape(panel, LANES)

        def kernel_rows(i, carry):
            first = i * many
            block = jnp.concatenate([slot(first + j) for j in range(many)], axis=0)
            affinity = lax.dot_general(
                block, columns, (((1,), (1,)), ((), ())), preferred_element_type=jnp.float32
            )
            kernel = jnp.exp2(affinity * slope - offset)
            for j in range(many):
                part = kernel[j * LANES : (j + 1) * LANES]
                kern[at, first + j] = part
                total = part[:, :LANES]
                for h in range(1, per_panel):
                    total = total + part[:, h * LANES : (h + 1) * LANES]
                if order:
                    total = total + tile_acc[first + j]
                if order < AY - 1:
                    tile_acc[first + j] = total
                else:
                    rows_mine[0, pl.ds(first + j, 1), :] = jnp.sum(total.T, axis=0, keepdims=True)
            return carry

        lax.fori_loop(0, side // many, kernel_rows, 0)
        if order == AY - 1:
            pair_rows(0, 0)
        lax.fori_loop(side // many, NB // many, kernel_rows, 0)
        if order == AY - 1:
            pair_rows(0, 1)

    def part_of(b, g):
        h = g % per_panel
        return kern[g // per_panel, b, :, h * LANES : (h + 1) * LANES]

    valid = lax.broadcasted_iota(jnp.int32, (side, LANES), 1) < rows_here
    scales = None
    for it in range(ITERS):
        if it:
            scale_rows = scales

            def scaled_rows(b, carry):
                total = part_of(b, 0) * scale_rows[0:1, :]
                for g in range(1, groups):
                    total = total + part_of(b, g) * scale_rows[g : g + 1, :]
                rows_mine[it, pl.ds(b, 1), :] = jnp.sum(total.T, axis=0, keepdims=True)
                return carry

            for half in range(2):
                lax.fori_loop(half * side, half * side + side, scaled_rows, 0, unroll=many)
                pair_rows(it, half)

        rows_phases = next(phases), next(phases)
        for half in range(2):
            view = pl.ds(half * side, side)
            arrived(rows_pair.at[it, view], pair_rows_phases[2 * it + half])
            rows_in[it, half, 0] = rows_mine[it, view] + rows_pair[it, view]
            for r in row_far[:-1]:
                send(rows_in.at[it, half, 0], rows_in.at[it, half, r], rows_phases[half], row_ids[r])
        if it == 0:
            def turn(b, carry):
                place = pl.ds(pl.multiple_of(b * LANES, LANES), LANES)
                toks_t[:, place] = slot(b).astype(jnp.float32).T.astype(jnp.bfloat16)
                return carry

            lax.fori_loop(0, NB, turn, 0, unroll=many)
        def weighted_columns(b, totals):
            spread = jnp.broadcast_to(weights[pl.ds(b, 1), :], (LANES, LANES)).T
            weight_cols[b] = spread
            return tuple(
                totals[g] + jnp.sum((part_of(b, g) * spread).reshape(LANES // 8, 8, LANES), axis=0)
                for g in range(groups)
            )

        zeros = tuple(jnp.zeros((8, LANES), jnp.float32) for _ in range(groups))
        totals = zeros
        for half in range(2):
            arrived(rows_in.at[it, half, pl.ds(1, NB - 1)], rows_phases[half])
            row_sum = jnp.sum(rows_in[it, half], axis=0)
            weights[pl.ds(half * side, side), :] = jnp.where(valid, 1.0 / row_sum, 0.0)
            totals = lax.fori_loop(half * side, half * side + side, weighted_columns, totals, unroll=many)
        for g in range(groups):
            cols_in[it, 0, g : g + 1, :] = jnp.sum(totals[g], axis=0, keepdims=True)
        col_phase = next(phases)
        if it < ITERS - 1:
            for r in far_first[:-1]:
                send(cols_in.at[it, 0], cols_in.at[it, r], col_phase, col_ids[r])

        if it == ITERS - 1:
            sums_phases = [next(phases) for _ in range(PARTS)]

            def send_sums(half, peers):
                for r in peers:
                    part = sums_out.at[col_peers[r][1], pl.ds(half * PART, PART)]
                    send(part, sums_in.at[half, r], sums_phases[half], col_ids[r])

            for step in reversed(steps):
                at = lax.rem(ya + step, AY)

                def assign_rows(b, carry):
                    spread = weight_cols[b].astype(jnp.bfloat16).astype(jnp.float32)
                    for h in range(per_panel):
                        lanes = slice(h * LANES, (h + 1) * LANES)
                        half_mat[step, b, :, lanes] = (kern[at, b, :, lanes] * spread).astype(jnp.bfloat16)
                    return carry

                lax.fori_loop(0, NB, assign_rows, 0, unroll=many)
                turned = jnp.dot(
                    toks_t[...],
                    half_mat[step].reshape(NB * LANES, panel),
                    preferred_element_type=jnp.float32,
                )
                for h in range(per_panel):
                    pair = turned[:, h * LANES : (h + 1) * LANES].T
                    sums_out[at * AZ + 2 * h] = pair[:HALF]
                    sums_out[at * AZ + 2 * h + 1] = pair[HALF:]
                send_sums(0, [r for r in far_first if r and r // AZ == step])
            for r in far_first[:-1]:
                send(cols_in.at[it, 0], cols_in.at[it, r], col_phase, col_ids[r])
            for half in range(1, PARTS):
                send_sums(half, far_first[:-1])
            for half in range(PARTS):
                sums_in[half, 0] = sums_out[mine_a, half * PART : (half + 1) * PART]

        arrived(cols_in.at[it, pl.ds(1, NA - 1)], col_phase)
        scales = col_mass / jnp.sum(cols_in[it], axis=0)

    last_scales = scales

    def plan_rows(b, carry):
        spread = weight_cols[b]
        for g in range(groups):
            h = g % per_panel
            half_mat[g // per_panel, b, :, h * LANES : (h + 1) * LANES] = (
                part_of(b, g) * spread * last_scales[g : g + 1, :]
            ).astype(jnp.bfloat16)
        return carry

    lax.fori_loop(0, NB, plan_rows, 0, unroll=many)

    new_phases = [next(phases) for _ in range(AY)]
    for half in range(PARTS):
        arrived(sums_in.at[half, pl.ds(1, NA - 1)], sums_phases[half])
        new_own = normalized_rows(jnp.sum(sums_in[half], axis=0))
        place = pl.ds(half * PART, PART)
        news[mine_a, place] = new_own.astype(jnp.bfloat16)
        for r in far_first[:-1]:
            send(news.at[mine_a, place], news.at[mine_a, place], new_phases[r // AZ], col_ids[r])
        new_ref[place, :] = new_own

    chunk = max(NB // SOFT_CHUNKS, 1)
    soft_phases = []
    firsts = [step * chunk for step in reversed(nearest_first(NB // chunk))]
    for order, step in enumerate(steps):
        at = panel_at[step]
        arrived(news.at[pl.ds(0, AZ - (step == 0))], new_phases[step])
        fresh = news[pl.ds(at * AZ, AZ)].reshape(panel, LANES)
        if order < AY - 1:

            def soft_rows(i, carry):
                place = pl.ds(i * many, many)
                block = jnp.dot(
                    half_mat[at, place].reshape(many * LANES, panel), fresh, preferred_element_type=jnp.float32
                ).reshape(many, LANES, LANES)
                tile_acc[place] = block if order == 0 else tile_acc[place] + block
                return carry

            lax.fori_loop(0, NB // many, soft_rows, 0)
            continue
        soft_phase = next(phases)

        def pass_on(first, phase):
            arrived(soft_pair.at[pl.ds(first, chunk)], phase)
            for r in reversed(range(first, first + chunk)):
                if r == 0:
                    soft_in[0] = soft[core, 0] + soft_pair[0]
                else:
                    soft_half[r] = soft[core, r] + soft_pair[r]
                    send(soft_half.at[r], soft_in.at[r], soft_phase, row_ids[r])

        for first in firsts:
            block = jnp.dot(
                jnp.concatenate([half_mat[at, row_peers[r][1]] for r in range(first, first + chunk)], axis=0),
                fresh,
                preferred_element_type=jnp.float32,
            )
            for r in range(first, first + chunk):
                whole = block[(r - first) * LANES : (r - first + 1) * LANES] + tile_acc[row_peers[r][1]]
                soft[0, r] = whole[:HALF]
                soft[1, r] = whole[HALF:]
            soft_phases.append((first, next(phases)))
            send(
                soft.at[1 - core, pl.ds(first, chunk)],
                soft_pair.at[pl.ds(first, chunk)],
                soft_phases[-1][1],
                sibling,
            )
            if len(soft_phases) > 1:
                pass_on(*soft_phases[-2])
        pass_on(*soft_phases[-1])
    arrived(soft_in.at[pl.ds(1, NB - 1)], soft_phase)
    soft_fin[core] = jnp.sum(soft_in[...], axis=0)
    phase = next(phases)
    send(soft_fin.at[core], soft_fin.at[core], phase, sibling)
    unit_tok = normalized_rows(tok_ref[...])
    arrived(soft_fin.at[0], phase)
    whole = jnp.concatenate([soft_fin[0], soft_fin[1]], axis=0)
    res_ref[...] = unit_tok - whole[:rows_here, :]
    for view, used in sent:
        pltpu.make_async_copy(view, view, send_sem.at[used]).wait()


def shards(dims, tokens, centroids):
    X, Y, Z, BY, BZ = dims
    AY, AZ = Y // BY, Z // BZ
    NB, NA = X * BY * BZ, AY * AZ
    panel = AZ * HALF
    groups = NA * HALF // LANES
    f32, bf16 = jnp.float32, jnp.bfloat16
    scratch = [
        pltpu.VMEM(tokens.shape, f32),
        pltpu.VMEM(centroids.shape, f32),
        pltpu.VMEM((2, NB, HALF, LANES), bf16),
        pltpu.VMEM((LANES, NB * LANES), bf16),
        pltpu.VMEM((NA, HALF, LANES), bf16),
        pltpu.VMEM((AY, NB, LANES, panel), f32),
        pltpu.VMEM((NB, LANES, LANES), f32),
        pltpu.VMEM((ITERS, NB, LANES), f32),
        pltpu.VMEM((ITERS, NB, LANES), f32),
        pltpu.VMEM((ITERS, 2, NB, NB // 2, LANES), f32),
        pltpu.VMEM((NB, LANES), f32),
        pltpu.VMEM((NB, LANES, LANES), f32),
        pltpu.VMEM((ITERS, NA, groups, LANES), f32),
        pltpu.VMEM((AY, NB, LANES, panel), bf16),
        pltpu.VMEM((NA, HALF, LANES), f32),
        pltpu.VMEM((PARTS, NA, PART, LANES), f32),
        pltpu.VMEM((NA, HALF, LANES), bf16),
        pltpu.VMEM((2, NB, HALF, LANES), f32),
        pltpu.VMEM((NB, HALF, LANES), f32),
        pltpu.VMEM((NB, HALF, LANES), f32),
        pltpu.VMEM((NB, HALF, LANES), f32),
        pltpu.VMEM((2, HALF, LANES), f32),
        pltpu.SemaphoreType.DMA((64,)),
        pltpu.SemaphoreType.DMA((64,)),
        pltpu.SemaphoreType.DMA((2,)),
    ]
    return pl.pallas_call(
        functools.partial(fused, dims),
        out_shape=(
            jax.ShapeDtypeStruct(centroids.shape, f32),
            jax.ShapeDtypeStruct(tokens.shape, f32),
        ),
        in_specs=[pl.BlockSpec(memory_space=pl.ANY)] * 2,
        out_specs=[pl.BlockSpec(memory_space=pltpu.VMEM)] * 2,
        scratch_shapes=scratch,
        compiler_params=pltpu.CompilerParams(
            collective_id=0, has_side_effects=True, vmem_limit_bytes=48 * 1024 * 1024
        ),
        name="kmeans_step",
    )(tokens, centroids)


def solution(mesh):
    in_specs = (P("dp", None), P(("dp", "cent"), None))
    out_specs = (P(("dp", "cent"), None), P("dp", None))
    dims = layout(mesh.shape["dp"])
    return jax.shard_map(
        functools.partial(shards, dims), mesh=mesh, in_specs=in_specs, out_specs=out_specs, check_vma=False
    )
```
